32 devices in a mesh: ctx: 8 (over z, x), head: 4 (over y, core).
Axes of the slice: x: 2, y: 2, z: 4, core: 2. Of those that a mesh axis runs over, the one named last changes fastest.
Arguments:
- queries: bfloat16 [1024, 64, 576], P('ctx', 'head'), may hold values from -104 to 104
- latent: bfloat16 [1024, 576], P('ctx'), may hold values from -6 to 6
- cotangent: bfloat16 [1024, 64, 512], P('ctx', 'head'), may hold values from -6 to 6
- selection: int32 [1024, 8], P('ctx'), may hold values from -1 to 15, as said below
Outputs:
- attended: bfloat16 [1024, 64, 512], P('ctx', 'head')
- grad_queries: bfloat16 [1024, 64, 576], P('ctx', 'head')
- grad_latent: float32 [1024, 576], P('ctx')
The draws below stay inside these ranges and needn't reach their ends.
Inputs may be any that keep to these rules, and one draw needn't show every extreme that they name: `selection`: row t lists distinct blocks, -1 in unused entries. It always lists the block of token t and never a later block. Call the 128 tokens of one index of the ctx axis a range. Besides blocks of its own range, a row lists at most one block of any other range; that range lies earlier, and all tokens of one 64-token block that list a block of a given range list the same one. So the tokens of one range list at most 2 blocks of another range. Rows of the last range always list a block of the first range. A row has unused entries only where fewer than 8 blocks are allowed by these rules.
All inputs are finite; a program needn't handle non-finite values.
Results may differ from the reference program's by a relative error of at most 0.03.
Values may be sent and summed in bfloat16 or wider, within the bound.
No kernel may reach another device: no remote copies, remote signals or barrier semaphores. Data moves between devices by JAX's collectives and lax.ppermute only.
A program may use at most 128 MiB of HBM per device.

```python
import jax
import jax.numpy as jnp
from jax import lax

DV = 512
BLOCK = 64
TOK_DEV = 128
LATENT = 576
HEADS = 64
SEQ = 1024
SEL = 8
N_CTX = 8


def block_picks(key):
    pick_key, rank_key = jax.random.split(jax.random.fold_in(key, 23))
    shards = SEQ // TOK_DEV
    pick = jax.random.randint(pick_key, (SEQ // BLOCK, shards), 0, TOK_DEV // BLOCK)
    return (pick, rank_key)


def joint_draw(key):
    base_key = jax.random.fold_in(key, 7)
    latent_key, query_key = jax.random.split(base_key, 2)
    shards = SEQ // TOK_DEV
    latent = jax.random.truncated_normal(latent_key, -6.0, 6.0, (SEQ, LATENT), jnp.float32)
    queries = jax.random.truncated_normal(query_key, -6.0, 6.0, (SEQ, HEADS, LATENT), jnp.float32)
    pick, unused_key = block_picks(key)
    first_sums = jnp.sum(latent[:TOK_DEV].reshape(TOK_DEV // BLOCK, BLOCK, LATENT), axis=1)
    last_tokens = jnp.arange((shards - 1) * TOK_DEV, SEQ, dtype=jnp.int32)
    target = first_sums[pick[last_tokens // BLOCK, 0]]
    queries = queries.at[(shards - 1) * TOK_DEV:].add(50.0 / LATENT * target[:, None, :])
    return (queries, latent)


def draw_queries(key, part):
    queries, latent = joint_draw(key)
    return queries.astype(jnp.bfloat16)


def draw_latent(key, part):
    queries, latent = joint_draw(key)
    return latent.astype(jnp.bfloat16)


def draw_selection(key, part):
    pick, rank_key = block_picks(key)
    shards = SEQ // TOK_DEV
    blocks_here = TOK_DEV // BLOCK
    block_count = SEQ // BLOCK
    token = jnp.arange(SEQ, dtype=jnp.int32)
    query_block = token // BLOCK
    query_shard = query_block // blocks_here
    key_block = jnp.arange(block_count, dtype=jnp.int32)
    key_shard = key_block // blocks_here
    chosen = pick[query_block[:, None], key_shard[None, :]]
    remote = (key_shard[None, :] < query_shard[:, None]) & (key_block[None, :] % blocks_here == chosen)
    nearby = (key_shard[None, :] == query_shard[:, None]) & (key_block[None, :] < query_block[:, None])
    itself = key_block[None, :] == query_block[:, None]
    forced = remote & (key_shard[None, :] == 0) & (query_shard[:, None] == shards - 1)
    rank = jax.random.randint(rank_key, (SEQ, block_count), 0, 65536)
    priority = jnp.where(itself | forced, 65536, jnp.where(remote | nearby, rank, -1))
    score = priority * block_count + key_block[None, :]
    best, where_best = lax.top_k(score, SEL)
    return jnp.where(best >= 0, where_best, -1).astype(jnp.int32)


def shard_levels(rng, extent, cuts, smallest, largest):
    level, own = 1.0, jax.random.fold_in(rng, 6)
    for dim, shards_of in cuts:
        steps = jnp.exp(jax.random.uniform(jax.random.fold_in(own, dim), (shards_of,), jnp.float32, smallest / len(cuts), largest / len(cuts)))
        level = level * jnp.repeat(steps, extent[dim] // shards_of).reshape([-1 if axis == dim else 1 for axis in range(len(extent))])
    return level


def normal_values(rng, shape, width, bound, pieces=(), kind=jnp.bfloat16):
    values = jax.random.normal(rng, shape, jnp.float32) * width
    if len(pieces) > 0:
        values = shard_levels(rng, shape, pieces, -0.22, 0.18) * values
    return jnp.clip(values, min=-bound, max=bound).astype(kind)


def setup_inputs(seed: int = 0) -> dict:
    key_of = jax.random.split(jax.random.key(seed), 5)
    queries = draw_queries(jax.random.fold_in(key_of[4], 71), 0)
    latent = draw_latent(jax.random.fold_in(key_of[4], 71), 0)
    cotangent = normal_values(key_of[2], (SEQ, HEADS, DV), 1.0, 6.0, ((0, 8), (1, 4)))
    selection = draw_selection(jax.random.fold_in(key_of[4], 71), 0)
    return {"queries": queries, "latent": latent, "cotangent": cotangent, "selection": selection}


softmax_scale = 192.0 ** -0.5


def block_table(chosen, my_shard, shards, blocks_here):
    tok_rows = chosen.shape[0]
    block_count = shards * blocks_here
    picked = jnp.any(chosen[:, :, None] == jnp.arange(block_count, dtype=jnp.int32)[None, None, :], axis=1)
    grouped = picked.reshape(tok_rows, shards, blocks_here)
    own_chosen = lax.dynamic_index_in_dim(grouped, my_shard, 1, keepdims=False)
    others = jnp.arange(shards, dtype=jnp.int32) != my_shard
    per_peer = jnp.any(grouped, axis=2) & others[None, :]
    query_block = jnp.arange(tok_rows, dtype=jnp.int32) // BLOCK
    same_slot = query_block[:, None] == jnp.arange(blocks_here, dtype=jnp.int32)[None, :]
    slot_chosen = (per_peer[:, :, None] & same_slot[:, None, :]).reshape(tok_rows, shards * blocks_here)
    requested = jnp.any(grouped.reshape(blocks_here, BLOCK, shards, blocks_here), axis=1)
    wanted = jnp.sum(jnp.where(requested, jnp.arange(blocks_here, dtype=jnp.int32)[None, None, :], 0), axis=2)
    wanted = jnp.where(others[None, :], wanted, 0).T.astype(jnp.int32)
    return own_chosen, slot_chosen, wanted


def key_mask(own_chosen, slot_chosen, block_len):
    tok_rows = own_chosen.shape[0]
    position = jnp.arange(tok_rows, dtype=jnp.int32)
    own_keys = jnp.repeat(own_chosen, block_len, axis=1) & (position[None, :] <= position[:, None])
    slot_keys = jnp.repeat(slot_chosen, block_len, axis=1)
    return jnp.concatenate([own_keys, slot_keys], axis=1)


def attend(query_rows, grad_rows, key_rows, allowed):
    value_width = grad_rows.shape[1]
    latent_width = key_rows.shape[1]
    values = key_rows[:, :value_width]
    scores = jnp.dot(query_rows, key_rows.T, preferred_element_type=jnp.float32) * softmax_scale
    masked = jnp.where(allowed, scores, -jnp.inf)
    row_max = jnp.max(masked, axis=1, keepdims=True)
    row_sum = jnp.sum(jnp.exp(masked - row_max), axis=1, keepdims=True)
    log_total = row_max + jnp.log(row_sum)
    weights = jnp.exp(masked - log_total)
    weights_low = weights.astype(jnp.bfloat16)
    result = jnp.dot(weights_low, values, preferred_element_type=jnp.float32).astype(jnp.bfloat16)
    row_delta = jnp.sum(grad_rows.astype(jnp.float32) * result.astype(jnp.float32), axis=1, keepdims=True)
    grad_weights = jnp.dot(grad_rows, values.T, preferred_element_type=jnp.float32)
    grad_scores = (softmax_scale * weights * (grad_weights - row_delta)).astype(jnp.bfloat16)
    grad_query = jnp.dot(grad_scores, key_rows, preferred_element_type=jnp.float32).astype(jnp.bfloat16)
    grad_keys = jnp.dot(grad_scores.T, query_rows, preferred_element_type=jnp.float32)
    grad_values = jnp.dot(weights_low.T, grad_rows, preferred_element_type=jnp.float32)
    grad_keys = grad_keys + jnp.pad(grad_values, ((0, 0), (0, latent_width - value_width)))
    return result, grad_query, grad_keys


def reference(queries, latent, cotangent, selection):
    seq_len, heads, latent_width = queries.shape
    value_width = cotangent.shape[2]
    shards = N_CTX
    tok_rows = seq_len // shards
    blocks_here = tok_rows // BLOCK
    latent_blocks = latent.reshape(shards * blocks_here, BLOCK, latent_width)

    def shard_step(running, my_shard):
        start = (my_shard * tok_rows).astype(jnp.int32)
        query_rows = lax.dynamic_slice_in_dim(queries, start, tok_rows, 0)
        grad_rows = lax.dynamic_slice_in_dim(cotangent, start, tok_rows, 0)
        chosen = lax.dynamic_slice_in_dim(selection, start, tok_rows, 0)
        own_chosen, slot_chosen, wanted = block_table(chosen, my_shard, shards, blocks_here)
        own_latent = lax.dynamic_slice_in_dim(latent, start, tok_rows, 0)
        starts = (jnp.arange(shards, dtype=jnp.int32)[:, None] * blocks_here + wanted).reshape(-1).astype(jnp.int32)
        fetched = jnp.take(latent_blocks, starts, axis=0).reshape(shards * blocks_here * BLOCK, latent_width)
        key_rows = jnp.concatenate([own_latent, fetched], axis=0)
        allowed = jnp.repeat(key_mask(own_chosen, slot_chosen, BLOCK), heads, axis=0)
        result, grad_query, grad_keys = attend(query_rows.reshape(tok_rows * heads, latent_width), grad_rows.reshape(tok_rows * heads, value_width), key_rows, allowed)
        spread = (wanted[:, :, None] == jnp.arange(blocks_here, dtype=jnp.int32)[None, None, :]).astype(jnp.float32)
        slot_grad = grad_keys[tok_rows:].reshape(shards, blocks_here, BLOCK, latent_width)
        dense_grad = jnp.sum(spread[:, :, :, None, None] * slot_grad[:, :, None, :, :], axis=1).reshape(seq_len, latent_width)
        placed = lax.dynamic_update_slice_in_dim(jnp.zeros((seq_len, latent_width), jnp.float32), grad_keys[:tok_rows], start, 0)
        outputs = (result.reshape(tok_rows, heads, value_width), grad_query.reshape(tok_rows, heads, latent_width))
        return running + dense_grad + placed, outputs

    zeros_init = jnp.zeros((seq_len, latent_width), jnp.float32)
    grad_latent, (results, grad_queries) = lax.scan(shard_step, zeros_init, jnp.arange(shards, dtype=jnp.int32))
    attended = results.reshape(seq_len, heads, value_width)
    grad_queries = grad_queries.reshape(seq_len, heads, latent_width)
    return (attended, grad_queries, grad_latent)
```

```python
import functools

import jax
import jax.numpy as jnp
from jax import lax
from jax.experimental import pallas as pl
from jax.experimental.pallas import tpu as pltpu
from jax.sharding import PartitionSpec as P

BLOCK = 64
TILE_ROWS = 512
MASKED = -1e30

softmax_scale = 192.0 ** (-0.5)

NT = (((1,), (1,)), ((), ()))
TN = (((0,), (0,)), ((), ()))


def dot(a, b, dims):
    return lax.dot_general(a, b, dims, preferred_element_type=jnp.float32)


def attention_kernel(n_far, blocks_here, heads, want_ref, q_ref, g_ref, own_ref, bias_ref, *rest):
    near = rest[:n_far]
    pair = rest[n_far : 2 * n_far]
    att_ref, gq_ref, keep_ref, send_ref, own_grad_ref = rest[2 * n_far : 2 * n_far + 5]
    scratch = rest[2 * n_far + 5 :]
    keys = scratch[:blocks_here]
    accs = scratch[blocks_here : 2 * blocks_here]
    dense_ref = scratch[2 * blocks_here]
    step = pl.program_id(0)
    steps = pl.num_programs(0)
    tile_rows = q_ref.shape[0]
    value_width = g_ref.shape[1]
    tiles_per_block = BLOCK * heads // tile_rows
    half = blocks_here // 2 * BLOCK
    far_rows = n_far * BLOCK
    my_half = want_ref[blocks_here, 0]

    @pl.when(step == 0)
    def _():
        for b in range(blocks_here):
            for k in range(n_far):
                block = want_ref[b, k]
                if half == BLOCK:
                    mine, other = near[k][...], pair[k][...]
                    side = block
                else:
                    offset = pl.multiple_of(lax.rem(block * BLOCK, half), BLOCK)
                    mine, other = near[k][pl.ds(offset, BLOCK), :], pair[k][pl.ds(offset, BLOCK), :]
                    side = lax.div(block * BLOCK, half)
                keys[b][k * BLOCK : (k + 1) * BLOCK, :] = jnp.where(side == my_half, mine, other)
            keys[b][far_rows:, :] = own_ref[: (b + 1) * BLOCK, :]
            accs[b][...] = jnp.zeros_like(accs[b])

    def tile(b):
        slots = n_far + b + 1
        query, grad = q_ref[...], g_ref[...]
        scores = dot(keys[b][...], query, NT) * softmax_scale
        scores = scores.reshape(slots, BLOCK, tile_rows) + bias_ref[:slots, :][:, None, :]
        first = lax.rem(step, tiles_per_block) * (tile_rows // heads)
        token = first + lax.div(lax.broadcasted_iota(jnp.int32, (1, BLOCK, tile_rows), 2), heads)
        place = lax.broadcasted_iota(jnp.int32, (1, BLOCK, tile_rows), 1)
        last = jnp.where(place <= token, scores[slots - 1 :], MASKED)
        scores = jnp.concatenate([scores[: slots - 1], last], axis=0).reshape(slots * BLOCK, tile_rows)
        top = jnp.max(scores, axis=0, keepdims=True)
        raised = jnp.exp(scores - top)
        total = jnp.sum(raised, axis=0, keepdims=True)
        grad_weights = dot(keys[b][:, :value_width], grad, NT)
        inverse = 1.0 / total
        weights = raised * inverse
        row_delta = jnp.sum(weights * grad_weights, axis=0, keepdims=True)
        grad_scores = (softmax_scale * weights * (grad_weights - row_delta)).astype(jnp.bfloat16)
        weights_low = weights.astype(jnp.bfloat16)
        accs[b][...] += dot(grad_scores, query, (((1,), (0,)), ((), ())))
        accs[b][:, :value_width] += dot(weights_low, grad, (((1,), (0,)), ((), ())))
        att_ref[...] = dot(weights_low, keys[b][:, :value_width], TN).astype(att_ref.dtype)
        gq_ref[...] = dot(grad_scores, keys[b][...], TN).astype(gq_ref.dtype)

    for b in range(blocks_here):
        pl.when(lax.div(step, tiles_per_block) == b)(functools.partial(tile, b))

    @pl.when(step == steps - 1)
    def _():
        dense_ref[...] = jnp.zeros_like(dense_ref)
        for b in range(blocks_here):
            for k in range(n_far):
                offset = pl.multiple_of(want_ref[b, k] * BLOCK, BLOCK)
                dense_ref[k, pl.ds(offset, BLOCK), :] += accs[b][k * BLOCK : (k + 1) * BLOCK, :]
        mine = pl.multiple_of(my_half * half, half)
        other = pl.multiple_of((1 - my_half) * half, half)
        for k in range(n_far):
            keep_ref[k, :, :] = dense_ref[k, pl.ds(mine, half), :].astype(keep_ref.dtype)
            send_ref[k, :, :] = dense_ref[k, pl.ds(other, half), :].astype(send_ref.dtype)
        for j in range(blocks_here):
            part = accs[j][far_rows + j * BLOCK : far_rows + (j + 1) * BLOCK, :]
            for b in range(j + 1, blocks_here):
                part = part + accs[b][far_rows + j * BLOCK : far_rows + (j + 1) * BLOCK, :]
            own_grad_ref[j * BLOCK : (j + 1) * BLOCK, :] = part


def attention(want, query_rows, grad_rows, own, bias, near, pair, heads, blocks_here):
    n_far = len(near)
    rows, latent_width = query_rows.shape
    value_width = grad_rows.shape[1]
    half = own.shape[0] // 2
    tile_rows = min(TILE_ROWS, BLOCK * heads)
    whole = lambda shape: pl.BlockSpec(shape, lambda i: (0,) * len(shape))
    by_tile = lambda width: pl.BlockSpec((tile_rows, width), lambda i: (i, 0))
    in_specs = [
        pl.BlockSpec(memory_space=pltpu.SMEM),
        by_tile(latent_width),
        by_tile(value_width),
        whole(own.shape),
        pl.BlockSpec((bias.shape[0], tile_rows), lambda i: (0, i)),
    ] + [whole((half, latent_width))] * (2 * n_far)
    out_shape = (
        jax.ShapeDtypeStruct((rows, value_width), jnp.bfloat16),
        jax.ShapeDtypeStruct((rows, latent_width), jnp.bfloat16),
        jax.ShapeDtypeStruct((n_far, half, latent_width), jnp.bfloat16),
        jax.ShapeDtypeStruct((n_far, half, latent_width), jnp.bfloat16),
        jax.ShapeDtypeStruct(own.shape, jnp.float32),
    )
    out_specs = (
        by_tile(value_width),
        by_tile(latent_width),
        whole((n_far, half, latent_width)),
        whole((n_far, half, latent_width)),
        whole(own.shape),
    )
    key_counts = [(n_far + b + 1) * BLOCK for b in range(blocks_here)]
    scratch = [pltpu.VMEM((count, latent_width), jnp.bfloat16) for count in key_counts]
    scratch += [pltpu.VMEM((count, latent_width), jnp.float32) for count in key_counts]
    scratch += [pltpu.VMEM((n_far, own.shape[0], latent_width), jnp.float32)]
    macs = rows * key_counts[-1] * 3 * (latent_width + value_width)
    return pl.pallas_call(
        functools.partial(attention_kernel, n_far, blocks_here, heads),
        grid=(rows // tile_rows,),
        in_specs=in_specs,
        out_specs=out_specs,
        out_shape=out_shape,
        scratch_shapes=scratch,
        compiler_params=pltpu.CompilerParams(vmem_limit_bytes=56 * 1024 * 1024),
        cost_estimate=pl.CostEstimate(
            flops=2 * macs,
            bytes_accessed=4 * rows * (latent_width + value_width),
            transcendentals=rows * key_counts[-1],
        ),
        name="attention",
    )(want, query_rows, grad_rows, own, bias, *near, *pair)


def slot_table(chosen, my_shard, shards, blocks_here):
    tok_rows = chosen.shape[0]
    valid = chosen >= 0
    owner = jnp.where(valid, chosen // blocks_here, -1)
    inside = jnp.where(valid, chosen % blocks_here, 0)
    target = my_shard - 1 - jnp.arange(shards - 1, dtype=jnp.int32)
    hit = (owner[None] == target[:, None, None]) & valid[None]
    far = jnp.any(hit, axis=2)
    want = jnp.max(
        jnp.where(hit, inside[None], 0).reshape(shards - 1, blocks_here, -1), axis=2
    ).T
    local = my_shard * blocks_here + jnp.arange(blocks_here, dtype=jnp.int32)
    near = jnp.any(chosen[None] == local[:, None, None], axis=2)
    allowed = jnp.concatenate([far, near], axis=0)
    return jnp.where(allowed, 0.0, MASKED).astype(jnp.float32), want.astype(jnp.int32)


def body(queries, latent, cotangent, selection):
    tok_rows, heads, latent_width = queries.shape
    value_width = cotangent.shape[2]
    shards = lax.axis_size("ctx")
    groups = lax.axis_size("head")
    my_shard = lax.axis_index("ctx")
    my_half = lax.axis_index("head") % 2
    blocks_here = tok_rows // BLOCK
    half = tok_rows // 2
    partner = [(i, i ^ 1) for i in range(groups)]

    part = lax.dynamic_slice_in_dim(latent, my_half * half, half, 0)
    near = [
        lax.ppermute(part, "ctx", [(i, i + k) for i in range(shards - k)]) for k in range(1, shards)
    ]
    pair = [lax.ppermute(rows, "head", partner) for rows in near]

    bias, want = slot_table(selection, my_shard, shards, blocks_here)
    bias = jnp.repeat(bias, heads, axis=1)
    want = jnp.concatenate([want, jnp.full((1, shards - 1), my_half, jnp.int32)], axis=0)
    attended, grad_queries, keep, send, own_grad = attention(
        want,
        queries.reshape(tok_rows * heads, latent_width),
        cotangent.reshape(tok_rows * heads, value_width),
        latent,
        bias,
        near,
        pair,
        heads,
        blocks_here,
    )

    got = lax.ppermute(send, "head", partner)
    own_keep = lax.dynamic_slice_in_dim(own_grad, my_half * half, half, 0)
    own_send = lax.dynamic_slice_in_dim(own_grad, (1 - my_half) * half, half, 0)
    total = own_keep + lax.ppermute(own_send, "head", partner)
    for k in range(1, shards):
        summed = (keep[k - 1].astype(jnp.float32) + got[k - 1].astype(jnp.float32)).astype(jnp.bfloat16)
        moved = lax.ppermute(summed, "ctx", [(i + k, i) for i in range(shards - k)])
        total = total + moved.astype(jnp.float32)
    low = total.astype(jnp.bfloat16)
    summed = low.astype(jnp.float32)
    for j in range(1, groups // 2):
        moved = lax.ppermute(low, "head", [(i, (i + 2 * j) % groups) for i in range(groups)])
        summed = summed + moved.astype(jnp.float32)
    other = lax.ppermute(summed, "head", partner)
    grad_latent = jnp.where(
        my_half == 0,
        jnp.concatenate([summed, other], axis=0),
        jnp.concatenate([other, summed], axis=0),
    )
    return (
        attended.reshape(tok_rows, heads, value_width),
        grad_queries.reshape(tok_rows, heads, latent_width),
        grad_latent,
    )


def solution(mesh):
    placed = (P("ctx", "head", None), P("ctx", None), P("ctx", "head", None), P("ctx", None))
    return jax.shard_map(
        body,
        mesh=mesh,
        in_specs=placed,
        out_specs=(P("ctx", "head", None), P("ctx", "head", None), P("ctx", None)),
        check_vma=False,
    )
```

```python
import functools

import jax
import jax.numpy as jnp
from jax import lax
from jax.experimental import pallas as pl
from jax.experimental.pallas import tpu as pltpu
from jax.sharding import PartitionSpec as P

BLOCK = 64
SCORE_ROWS = 512
OUT_ROWS = 1024
MASKED = -1e30
WIDE_ROWS = 256
VMEM_BYTES = 32 * 1024 * 1024
WIDE_BYTES = 60 * 1024 * 1024
UNROLLED = 1 << 21

softmax_scale = 192.0 ** (-0.5)
EXP2_SCALE = softmax_scale * 1.4426950408889634

NN = (((1,), (0,)), ((), ()))
NT = (((1,), (1,)), ((), ()))
TN = (((0,), (0,)), ((), ()))


def dot(a, b, dims):
    return lax.dot_general(a, b, dims, preferred_element_type=jnp.float32)


def per_block(blocks_here, tile_rows, heads, tile):
    which = lax.div(pl.program_id(0), BLOCK * heads // tile_rows)
    for b in range(blocks_here):
        pl.when(which == b)(functools.partial(tile, b))


def spread_slots(dense_ref, acc_ref, want_ref, slots):
    dense_ref[...] = jnp.zeros_like(dense_ref)
    for b in range(acc_ref.shape[0]):
        for at, slot in enumerate(slots):
            offset = pl.multiple_of(want_ref[b, slot] * BLOCK, BLOCK)
            dense_ref[at, pl.ds(offset, BLOCK), :] += acc_ref[b, slot * BLOCK : (slot + 1) * BLOCK, :]


def write_halves(dense_ref, at, my_half, keep_ref, send_ref):
    half = keep_ref.shape[1]
    mine = pl.multiple_of(my_half * half, half)
    other = pl.multiple_of((1 - my_half) * half, half)
    for i in range(keep_ref.shape[0]):
        keep_ref[i, :, :] = dense_ref[at + i, pl.ds(mine, half), :].astype(keep_ref.dtype)
        send_ref[i, :, :] = dense_ref[at + i, pl.ds(other, half), :].astype(send_ref.dtype)


def table_kernel(n_far, heads, place_ref, chosen_ref, bias_ref, want_ref):
    tok_rows = chosen_ref.shape[1]
    blocks_here = tok_rows // BLOCK
    my_shard = place_ref[0]
    chosen = chosen_ref[...]
    valid = chosen >= 0
    owner = jnp.where(valid, lax.div(chosen, blocks_here), -1)
    inside = chosen - owner * blocks_here
    allowed = []
    for slot in range(n_far):
        target = place_ref[2 + slot]
        hit = (owner == target) & valid & (target != my_shard)
        allowed.append(jnp.max(hit.astype(jnp.float32), axis=0, keepdims=True))
        want = jnp.max(jnp.where(hit, inside, 0), axis=0, keepdims=True)
        for b in range(blocks_here):
            want_ref[b, slot] = jnp.max(want[:, b * BLOCK : (b + 1) * BLOCK])
        want_ref[blocks_here, slot] = place_ref[1]
    for j in range(blocks_here):
        hit = valid & (chosen == my_shard * blocks_here + j)
        allowed.append(jnp.max(hit.astype(jnp.float32), axis=0, keepdims=True))
    rows = tok_rows * heads
    token = lax.div(lax.broadcasted_iota(jnp.int32, (tok_rows, rows), 1), heads)
    spread = token == lax.broadcasted_iota(jnp.int32, (tok_rows, rows), 0)
    allowed = jnp.concatenate(allowed, axis=0).astype(jnp.bfloat16)
    by_row = dot(allowed, jnp.where(spread, 1.0, 0.0).astype(jnp.bfloat16), NN)
    bias_ref[...] = jnp.where(by_row > 0.5, 0.0, MASKED)


def join_kernel(*refs):
    out_ref = refs[-1]
    for i, ref in enumerate(refs[:-1]):
        out_ref[i : i + 1, :, :] = ref[...]


def place_slots(keys_ref, want_ref, first_slot, mine_ref, other_ref, skip, my_half, half):
    for b in range(keys_ref.shape[0]):
        for slot in range(mine_ref.shape[0] - skip):
            block = want_ref[b, first_slot + slot]
            offset = pl.multiple_of(lax.rem(block * BLOCK, half), BLOCK)
            mine = mine_ref[skip + slot, pl.ds(offset, BLOCK), :]
            other = other_ref[skip + slot, pl.ds(offset, BLOCK), :]
            picked = jnp.where(lax.div(block * BLOCK, half) == my_half, mine, other)
            keys_ref[b, slot * BLOCK : (slot + 1) * BLOCK, :] = picked


def each_tile(blocks_here, heads, tile_rows, steps, run):
    block_rows = BLOCK * heads
    if steps == 1:
        run([(b, b * block_rows + at, at) for b in range(blocks_here) for at in range(0, block_rows, tile_rows)])
        return
    step = pl.program_id(0)
    at = lax.rem(step, block_rows // tile_rows) * tile_rows
    for b in range(blocks_here):
        pl.when(lax.div(step, block_rows // tile_rows) == b)(functools.partial(run, [(b, 0, at)]))


def early_kernel(n_cross, blocks_here, heads, tile_rows, steps, want_ref, q_ref, g_ref, own_ref, mine_ref, other_ref, keys_ref, scores_ref, gw_ref, grad_ref):
    value_width = g_ref.shape[1]
    half = blocks_here // 2 * BLOCK
    n_direct = mine_ref.shape[0] - 1

    def start():
        place_slots(keys_ref, want_ref, n_cross, mine_ref, other_ref, 1, want_ref[blocks_here, 0], half)
        for b in range(blocks_here):
            keys_ref[b, n_direct * BLOCK :, :] = own_ref[...]

    def run(tiles):
        for b, local, _ in tiles:
            count = (n_direct + b + 1) * BLOCK
            here = slice(local, local + tile_rows)
            scores_ref[:count, here] = dot(keys_ref[b, :count, :], q_ref[here, :], NT)
            gw_ref[:count, here] = dot(keys_ref[b, :count, :value_width], g_ref[here, :], NT)

    at_step(0, steps, start)
    grad_ref[...] = g_ref[...]
    each_tile(blocks_here, heads, tile_rows, steps, run)


def at_step(which, steps, fn):
    if steps == 1:
        fn()
    else:
        pl.when(pl.program_id(0) == which)(fn)


def score_kernel(n_far, n_cross, blocks_here, heads, tile_rows, steps, want_ref, q_ref, g_ref, bias_ref, early_keys_ref, early_scores_ref, early_gw_ref, mine_ref, other_ref, weights_ref, grads_ref, keys_ref, keep_ref, send_ref, late_keep_ref, late_send_ref, acc_ref, dense_ref):
    value_width = g_ref.shape[1]
    half = blocks_here // 2 * BLOCK
    cross_rows = n_cross * BLOCK
    my_half = want_ref[blocks_here, 0]
    far_rows = n_far * BLOCK

    def start():
        place_slots(keys_ref, want_ref, 0, mine_ref, other_ref, 0, my_half, half)
        keys_ref[:, cross_rows:, :] = early_keys_ref[...]
        if steps > 1:
            acc_ref[...] = jnp.zeros_like(acc_ref)

    def window(tile):
        b, local, _ = tile
        return n_far + b + 1, slice(local, local + tile_rows)

    def products(tile):
        here = window(tile)[1]
        keys = keys_ref[tile[0], :cross_rows, :]
        scores = dot(keys, q_ref[here, :], NT)
        grad_weights = dot(keys[:, :value_width], g_ref[here, :], NT)
        return scores, grad_weights

    def finish(tile, scores, grad_weights):
        b, _, at = tile
        slots, here = window(tile)
        count = slots * BLOCK
        early = count - cross_rows
        scores = jnp.concatenate([scores, early_scores_ref[:early, here]], axis=0)
        grad_weights = jnp.concatenate([grad_weights, early_gw_ref[:early, here]], axis=0)
        scores = scores.reshape(slots, BLOCK, tile_rows)
        token = lax.div(at, heads) + lax.div(lax.broadcasted_iota(jnp.int32, (1, BLOCK, tile_rows), 2), heads)
        place = lax.broadcasted_iota(jnp.int32, (1, BLOCK, tile_rows), 1)
        last = jnp.where(place <= token, scores[slots - 1 :], MASKED)
        scores = jnp.concatenate([scores[: slots - 1], last], axis=0)
        bias = bias_ref[:slots, here]
        top = jnp.max(jnp.max(scores, axis=1) * EXP2_SCALE + bias, axis=0, keepdims=True)
        raised = jnp.exp2(scores * EXP2_SCALE + (bias - top)[:, None, :]).reshape(count, tile_rows)
        total = jnp.sum(raised, axis=0, keepdims=True)
        weights = raised * (1.0 / total)
        row_delta = jnp.sum(weights * grad_weights, axis=0, keepdims=True)
        grad_scores = (weights * (grad_weights - row_delta)).astype(jnp.bfloat16)
        weights_low = weights.astype(jnp.bfloat16)
        weights_ref[:count, here] = weights_low
        grads_ref[:count, here] = grad_scores
        query_part = dot(grad_scores[:far_rows], q_ref[here, :], NN) * softmax_scale
        grad_part = dot(weights_low[:far_rows], g_ref[here, :], NN)
        if steps == 1 and at == 0:
            acc_ref[b, :, :] = query_part
        else:
            acc_ref[b, :, :] += query_part
        acc_ref[b, :, :value_width] += grad_part

    def run(tiles):
        ready = products(tiles[0])
        for i, tile in enumerate(tiles):
            coming = products(tiles[i + 1]) if i + 1 < len(tiles) else None
            finish(tile, *ready)
            ready = coming

    def end():
        spread_slots(dense_ref, acc_ref, want_ref, list(range(1, n_cross)) + [0] + list(range(n_cross, n_far)))
        write_halves(dense_ref, 0, my_half, keep_ref, send_ref)
        write_halves(dense_ref, n_cross - 1, my_half, late_keep_ref, late_send_ref)

    at_step(0, steps, start)
    each_tile(blocks_here, heads, tile_rows, steps, run)
    at_step(steps - 1, steps, end)


def grad_kernel(n_far, blocks_here, heads, want_ref, q_ref, g_ref, weights_ref, grads_ref, keep_ref, send_ref, acc_ref, dense_ref):
    value_width = g_ref.shape[1]
    start = n_far * BLOCK
    block_rows = BLOCK * heads
    for b in range(blocks_here):
        count = (b + 1) * BLOCK
        here = slice(b * block_rows, (b + 1) * block_rows)
        acc_ref[b, :count, :] = dot(grads_ref[start : start + count, here], q_ref[here, :], NN) * softmax_scale
        acc_ref[b, :count, :value_width] += dot(weights_ref[start : start + count, here], g_ref[here, :], NN)
    for j in range(blocks_here):
        rows = slice(j * BLOCK, (j + 1) * BLOCK)
        part = acc_ref[j, rows, :]
        for b in range(j + 1, blocks_here):
            part = part + acc_ref[b, rows, :]
        dense_ref[0, rows, :] = part
    write_halves(dense_ref, 0, want_ref[blocks_here, 0], keep_ref, send_ref)


def out_kernel(n_far, blocks_here, heads, keys_ref, weights_ref, grads_ref, att_ref, gq_ref):
    tile_rows, value_width = att_ref.shape

    def tile(b):
        count = (n_far + b + 1) * BLOCK
        att_ref[...] = dot(weights_ref[:count, :], keys_ref[b, :count, :value_width], TN).astype(att_ref.dtype)
        product = dot(grads_ref[:count, :], keys_ref[b, :count, :], TN)
        gq_ref[...] = (product * softmax_scale).astype(gq_ref.dtype)

    per_block(blocks_here, tile_rows, heads, tile)


def whole(shape):
    return pl.BlockSpec(shape, lambda i: (0,) * len(shape))


def rows_of(tile_rows, width):
    return pl.BlockSpec((tile_rows, width), lambda i: (i, 0))


def lanes_of(count, tile_rows):
    return pl.BlockSpec((count, tile_rows), lambda i: (0, i))


def call(kernel, grid, in_specs, out_specs, out_shape, scratch, macs, moved, name):
    return pl.pallas_call(
        kernel,
        grid=(grid,),
        in_specs=in_specs,
        out_specs=out_specs,
        out_shape=out_shape,
        scratch_shapes=scratch,
        compiler_params=pltpu.CompilerParams(vmem_limit_bytes=VMEM_BYTES),
        cost_estimate=pl.CostEstimate(flops=2 * macs, bytes_accessed=moved, transcendentals=0),
        name=name,
    )


def whole_call(kernel, in_specs, out_specs, out_shape, scratch, macs, moved, name, steps=1):
    in_vmem = pl.BlockSpec(memory_space=pltpu.VMEM)
    if steps == 1:
        in_specs, out_specs, grid = [in_vmem] * len(in_specs), (in_vmem,) * len(out_specs), {}
    else:
        grid = {"grid": (steps,)}
    return pl.pallas_call(
        kernel,
        in_specs=[pl.BlockSpec(memory_space=pltpu.SMEM)] + list(in_specs),
        out_specs=tuple(out_specs),
        out_shape=out_shape,
        scratch_shapes=scratch,
        compiler_params=pltpu.CompilerParams(
            vmem_limit_bytes=VMEM_BYTES if steps == 1 else WIDE_BYTES
        ),
        cost_estimate=pl.CostEstimate(flops=2 * macs, bytes_accessed=moved, transcendentals=0),
        name=name,
        **grid,
    )


def tiling(rows, keys, heads):
    if rows * keys <= UNROLLED:
        return min(SCORE_ROWS, BLOCK * heads), 1
    tile_rows = min(WIDE_ROWS, BLOCK * heads)
    return tile_rows, rows // tile_rows


def table_call(place, chosen, n_far, heads):
    tok_rows = chosen.shape[1]
    blocks_here = tok_rows // BLOCK
    smem = pl.BlockSpec(memory_space=pltpu.SMEM)
    in_vmem = pl.BlockSpec(memory_space=pltpu.VMEM)
    return pl.pallas_call(
        functools.partial(table_kernel, n_far, heads),
        in_specs=[smem, in_vmem],
        out_specs=(in_vmem, smem),
        out_shape=(
            jax.ShapeDtypeStruct((n_far + blocks_here, tok_rows * heads), jnp.float32),
            jax.ShapeDtypeStruct((blocks_here + 1, n_far), jnp.int32),
        ),
        compiler_params=pltpu.CompilerParams(vmem_limit_bytes=VMEM_BYTES),
        name="table",
    )(place, chosen)


def join_call(pieces):
    in_vmem = pl.BlockSpec(memory_space=pltpu.VMEM)
    return pl.pallas_call(
        join_kernel,
        in_specs=[in_vmem] * len(pieces),
        out_specs=in_vmem,
        out_shape=jax.ShapeDtypeStruct((len(pieces),) + pieces[0].shape[1:], pieces[0].dtype),
        compiler_params=pltpu.CompilerParams(vmem_limit_bytes=VMEM_BYTES),
        name="join",
    )(*pieces)


def early_call(want, query_rows, grad_rows, own, mine, other, n_cross, n_far, heads):
    rows, width = query_rows.shape
    value_width = grad_rows.shape[1]
    tok_rows = own.shape[0]
    blocks_here = tok_rows // BLOCK
    keys = (mine.shape[0] - 1) * BLOCK + tok_rows
    tile_rows, steps = tiling(rows, n_far * BLOCK + tok_rows, heads)
    key_shape = (blocks_here, keys, width)
    by_row = [rows_of(tile_rows, width), rows_of(tile_rows, value_width)]
    return whole_call(
        functools.partial(early_kernel, n_cross, blocks_here, heads, tile_rows, steps),
        by_row + [whole(own.shape), whole(mine.shape), whole(other.shape)],
        [whole(key_shape), lanes_of(keys, tile_rows), lanes_of(keys, tile_rows), by_row[1]],
        (
            jax.ShapeDtypeStruct(key_shape, jnp.bfloat16),
            jax.ShapeDtypeStruct((keys, rows), jnp.float32),
            jax.ShapeDtypeStruct((keys, rows), jnp.float32),
            jax.ShapeDtypeStruct((rows, value_width), jnp.bfloat16),
        ),
        [],
        rows * keys * (width + value_width),
        rows * (width + value_width) * 4,
        "early_scores",
        steps,
    )(want, query_rows, grad_rows, own, mine, other)


def score_call(want, query_rows, grad_rows, bias, early, mine, other, n_far, heads, tok_rows):
    rows, width = query_rows.shape
    value_width = grad_rows.shape[1]
    blocks_here = tok_rows // BLOCK
    n_cross = mine.shape[0]
    keys = n_far * BLOCK + tok_rows
    tile_rows, steps = tiling(rows, keys, heads)
    now = jax.ShapeDtypeStruct((n_cross - 1, tok_rows // 2, width), jnp.bfloat16)
    late = jax.ShapeDtypeStruct((n_far - n_cross + 1, tok_rows // 2, width), jnp.bfloat16)
    early_keys = early[0].shape[1]
    key_shape = (blocks_here, keys, width)
    return whole_call(
        functools.partial(score_kernel, n_far, n_cross, blocks_here, heads, tile_rows, steps),
        [
            rows_of(tile_rows, width),
            rows_of(tile_rows, value_width),
            lanes_of(bias.shape[0], tile_rows),
            whole(early[0].shape),
            lanes_of(early_keys, tile_rows),
            lanes_of(early_keys, tile_rows),
            whole(mine.shape),
            whole(other.shape),
        ],
        [lanes_of(keys, tile_rows), lanes_of(keys, tile_rows), whole(key_shape)]
        + [whole(s.shape) for s in (now, now, late, late)],
        (
            jax.ShapeDtypeStruct((keys, rows), jnp.bfloat16),
            jax.ShapeDtypeStruct((keys, rows), jnp.bfloat16),
            jax.ShapeDtypeStruct(key_shape, jnp.bfloat16),
            now,
            now,
            late,
            late,
        ),
        [
            pltpu.VMEM((blocks_here, n_far * BLOCK, width), jnp.float32),
            pltpu.VMEM((n_far, tok_rows, width), jnp.float32),
        ],
        rows * keys * 2 * (width + value_width),
        rows * (width + value_width) * 4,
        "scores",
        steps,
    )(want, query_rows, grad_rows, bias, *early, mine, other)


def grad_call(want, query_rows, grad_rows, weights, grads, n_far, heads, tok_rows):
    rows, width = query_rows.shape
    value_width = grad_rows.shape[1]
    blocks_here = tok_rows // BLOCK
    half = jax.ShapeDtypeStruct((1, tok_rows // 2, width), jnp.bfloat16)
    return whole_call(
        functools.partial(grad_kernel, n_far, blocks_here, heads),
        [None] * 4,
        [None] * 2,
        (half, half),
        [
            pltpu.VMEM((blocks_here, tok_rows, width), jnp.float32),
            pltpu.VMEM((1, tok_rows, width), jnp.float32),
        ],
        rows * tok_rows * (width + value_width),
        rows * (width + value_width) * 4,
        "own_grads",
    )(want, query_rows, grad_rows, weights, grads)


def out_call(keys, weights, grads, n_far, heads, value_width):
    blocks_here, count, width = keys.shape
    rows = weights.shape[1]
    tile_rows = min(OUT_ROWS if rows * count <= UNROLLED else WIDE_ROWS, BLOCK * heads)
    return call(
        functools.partial(out_kernel, n_far, blocks_here, heads),
        rows // tile_rows,
        [whole(keys.shape), lanes_of(count, tile_rows), lanes_of(count, tile_rows)],
        (rows_of(tile_rows, value_width), rows_of(tile_rows, width)),
        (
            jax.ShapeDtypeStruct((rows, value_width), jnp.bfloat16),
            jax.ShapeDtypeStruct((rows, width), jnp.bfloat16),
        ),
        [],
        rows * count * (width + value_width),
        rows * (width + value_width) * 4,
        "outputs",
    )(keys, weights, grads)


def body(queries, latent, cotangent, selection):
    tok_rows, heads, width = queries.shape
    value_width = cotangent.shape[2]
    shards = lax.axis_size("ctx")
    groups = lax.axis_size("head")
    my_shard = lax.axis_index("ctx")
    my_half = lax.axis_index("head") % 2
    blocks_here = tok_rows // BLOCK
    half = tok_rows // 2
    lines = shards // 2
    partner = [(i, i ^ 1) for i in range(groups)]
    across = [(i, i ^ 1) for i in range(shards)]

    def swap(rows):
        return lax.ppermute(rows, "head", partner)

    def up(rows, hops):
        return lax.ppermute(rows, "ctx", [(i, i + 2 * hops) for i in range(shards - 2 * hops)])

    def down(rows, hops):
        return lax.ppermute(rows, "ctx", [(i + 2 * hops, i) for i in range(shards - 2 * hops)])

    offsets = sorted(range(1, lines), key=lambda k: (k != 2, k))
    cross_target = (my_shard ^ 1) - 2 * jnp.array([0] + offsets, jnp.int32)
    direct_target = my_shard - 2 * jnp.array(offsets, jnp.int32)
    n_cross, n_far = lines, shards - 1
    place = jnp.concatenate(
        [jnp.stack([my_shard, my_half]).astype(jnp.int32), cross_target, direct_target]
    )
    grad_rows = cotangent.reshape(tok_rows * heads, value_width)

    held = lax.dynamic_slice_in_dim(latent, my_half * half, half, 0)[None]
    pieces = [held] + [up(held, k) for k in offsets]
    bias, want = table_call(place, selection.T, n_far, heads)
    *pieces, bias, want, queries = lax.optimization_barrier((*pieces, bias, want, queries))
    mine = join_call(pieces)
    mine, queries = lax.optimization_barrier((mine, queries))
    cross = lax.ppermute(mine, "ctx", across)
    query_rows = queries.reshape(tok_rows * heads, width)
    *early, grad_rows = early_call(
        want, query_rows, grad_rows, latent, mine, swap(mine), n_cross, n_far, heads
    )
    cross, early[1] = lax.optimization_barrier((cross, early[1]))
    weights, grads, keys, keep, send, late_keep, late_send = score_call(
        want, query_rows, grad_rows, bias, early, cross, swap(cross), n_far, heads, tok_rows
    )

    moving = (keep.astype(jnp.float32) + swap(send).astype(jnp.float32)).astype(jnp.bfloat16)
    moving, weights, late_send = lax.optimization_barrier((moving, weights, late_send))
    arrived = lax.ppermute(moving, "ctx", across)
    attended, grad_queries = out_call(keys, weights, grads, n_far, heads, value_width)
    late = late_keep.astype(jnp.float32) + swap(late_send).astype(jnp.float32)
    total = (late[1:] + arrived.astype(jnp.float32)).astype(jnp.bfloat16)
    late_own = late[:1].astype(jnp.bfloat16)
    total, late_own, grad_queries, weights = lax.optimization_barrier((total, late_own, grad_queries, weights))
    grad_queries = grad_queries.reshape(tok_rows, heads, width).transpose(1, 2, 0)
    moved = [down(total[i : i + 1], k) for i, k in enumerate(offsets)]
    keep, send = grad_call(want, query_rows, grad_rows, weights, grads, n_far, heads, tok_rows)
    total = keep.astype(jnp.float32) + swap(send).astype(jnp.float32)
    total = total + lax.ppermute(late_own, "ctx", across).astype(jnp.float32)
    for part in moved:
        total = total + part.astype(jnp.float32)
    low = total[0].astype(jnp.bfloat16)
    low, grad_queries = lax.optimization_barrier((low, grad_queries))
    summed = low.astype(jnp.float32)
    for j in range(1, groups // 2):
        moved = lax.ppermute(low, "head", [(i, (i + 2 * j) % groups) for i in range(groups)])
        summed = summed + moved.astype(jnp.float32)
    rest = swap(summed)
    grad_latent = jnp.where(
        my_half == 0,
        jnp.concatenate([summed, rest], axis=0),
        jnp.concatenate([rest, summed], axis=0),
    )
    return (
        attended.reshape(tok_rows, heads, value_width),
        grad_queries.transpose(2, 0, 1),
        grad_latent,
    )


def solution(mesh):
    placed = (P("ctx", "head", None), P("ctx", None), P("ctx", "head", None), P("ctx", None))
    return jax.shard_map(
        body,
        mesh=mesh,
        in_specs=placed,
        out_specs=(P("ctx", "head", None), P("ctx", "head", None), P("ctx", None)),
        check_vma=False,
    )
```

```python
import functools

import jax
import jax.numpy as jnp
from jax import lax
from jax.experimental import pallas as pl
from jax.experimental.pallas import tpu as pltpu
from jax.sharding import PartitionSpec as P

BLOCK = 64
SCORE_ROWS = 512
OUT_ROWS = 1024
MASKED = -1e30
WIDE_ROWS = 256
VMEM_BYTES = 32 * 1024 * 1024
WIDE_BYTES = 60 * 1024 * 1024
UNROLLED = 1 << 21

softmax_scale = 192.0 ** (-0.5)
EXP2_SCALE = softmax_scale * 1.4426950408889634

NN = (((1,), (0,)), ((), ()))
NT = (((1,), (1,)), ((), ()))
TN = (((0,), (0,)), ((), ()))


def dot(a, b, dims):
    return lax.dot_general(a, b, dims, preferred_element_type=jnp.float32)


def per_block(blocks_here, tile_rows, heads, tile):
    which = lax.div(pl.program_id(0), BLOCK * heads // tile_rows)
    for b in range(blocks_here):
        pl.when(which == b)(functools.partial(tile, b))


def spread_slots(dense_ref, acc_ref, want_ref, slots):
    dense_ref[...] = jnp.zeros_like(dense_ref)
    for b in range(acc_ref.shape[0]):
        for at, slot in enumerate(slots):
            offset = pl.multiple_of(want_ref[b, slot] * BLOCK, BLOCK)
            dense_ref[at, pl.ds(offset, BLOCK), :] += acc_ref[b, slot * BLOCK : (slot + 1) * BLOCK, :]


def write_halves(dense_ref, at, my_half, keep_ref, send_ref):
    half = keep_ref.shape[1]
    for i in range(keep_ref.shape[0]):
        turned = dense_ref[at + i, :, :].astype(keep_ref.dtype).T
        first, second = turned[:half, :], turned[half:, :]
        keep_ref[i, :, :] = jnp.where(my_half == 0, first, second)
        send_ref[i, :, :] = jnp.where(my_half == 0, second, first)


def table_kernel(n_far, heads, place_ref, chosen_ref, bias_ref, want_ref):
    tok_rows = chosen_ref.shape[1]
    blocks_here = tok_rows // BLOCK
    my_shard = place_ref[0]
    chosen = chosen_ref[...]
    valid = chosen >= 0
    owner = jnp.where(valid, lax.div(chosen, blocks_here), -1)
    inside = chosen - owner * blocks_here
    allowed = []
    for slot in range(n_far):
        target = place_ref[2 + slot]
        hit = (owner == target) & valid & (target != my_shard)
        allowed.append(jnp.max(hit.astype(jnp.float32), axis=0, keepdims=True))
        want = jnp.max(jnp.where(hit, inside, 0), axis=0, keepdims=True)
        for b in range(blocks_here):
            want_ref[b, slot] = jnp.max(want[:, b * BLOCK : (b + 1) * BLOCK])
        want_ref[blocks_here, slot] = place_ref[1]
    for j in range(blocks_here):
        hit = valid & (chosen == my_shard * blocks_here + j)
        allowed.append(jnp.max(hit.astype(jnp.float32), axis=0, keepdims=True))
    rows = tok_rows * heads
    token = lax.div(lax.broadcasted_iota(jnp.int32, (tok_rows, rows), 1), heads)
    spread = token == lax.broadcasted_iota(jnp.int32, (tok_rows, rows), 0)
    allowed = jnp.concatenate(allowed, axis=0).astype(jnp.bfloat16)
    by_row = dot(allowed, jnp.where(spread, 1.0, 0.0).astype(jnp.bfloat16), NN)
    bias_ref[...] = jnp.where(by_row > 0.5, 0.0, MASKED)


def join_kernel(*refs):
    out_ref = refs[-1]
    for i, ref in enumerate(refs[:-1]):
        out_ref[i : i + 1, :, :] = ref[...]


def place_slots(keys_ref, rows_ref, want_ref, first_slot, mine_ref, other_ref, skip, my_half):
    for slot in range(mine_ref.shape[0] - skip):
        mine, other = mine_ref[skip + slot, :, :], other_ref[skip + slot, :, :]
        turned = jnp.concatenate(
            [jnp.where(my_half == 0, mine, other), jnp.where(my_half == 0, other, mine)], axis=0
        )
        rows_ref[slot, :, :] = turned.T
        for b in range(keys_ref.shape[0]):
            offset = pl.multiple_of(want_ref[b, first_slot + slot] * BLOCK, BLOCK)
            keys_ref[b, slot * BLOCK : (slot + 1) * BLOCK, :] = rows_ref[slot, pl.ds(offset, BLOCK), :]


def each_tile(blocks_here, heads, tile_rows, steps, run):
    block_rows = BLOCK * heads
    if steps == 1:
        run([(b, b * block_rows + at, at) for b in range(blocks_here) for at in range(0, block_rows, tile_rows)])
        return
    step = pl.program_id(0)
    at = lax.rem(step, block_rows // tile_rows) * tile_rows
    for b in range(blocks_here):
        pl.when(lax.div(step, block_rows // tile_rows) == b)(functools.partial(run, [(b, 0, at)]))


def early_kernel(n_cross, blocks_here, heads, tile_rows, steps, want_ref, q_ref, g_ref, own_ref, mine_ref, other_ref, keys_ref, scores_ref, gw_ref, grad_ref, rows_ref):
    value_width = g_ref.shape[1]
    n_direct = mine_ref.shape[0] - 1

    def start():
        place_slots(keys_ref, rows_ref, want_ref, n_cross, mine_ref, other_ref, 1, want_ref[blocks_here, 0])
        own = own_ref[...].T
        for b in range(blocks_here):
            keys_ref[b, n_direct * BLOCK :, :] = own

    def run(tiles):
        for b, local, _ in tiles:
            count = (n_direct + b + 1) * BLOCK
            here = slice(local, local + tile_rows)
            scores_ref[:count, here] = dot(keys_ref[b, :count, :], q_ref[here, :], NT)
            gw_ref[:count, here] = dot(keys_ref[b, :count, :value_width], g_ref[here, :], NT)

    at_step(0, steps, start)
    grad_ref[...] = g_ref[...]
    each_tile(blocks_here, heads, tile_rows, steps, run)


def at_step(which, steps, fn):
    if steps == 1:
        fn()
    else:
        pl.when(pl.program_id(0) == which)(fn)


def score_kernel(n_far, n_cross, blocks_here, heads, tile_rows, steps, want_ref, q_ref, g_ref, bias_ref, early_keys_ref, early_scores_ref, early_gw_ref, mine_ref, other_ref, weights_ref, grads_ref, keys_ref, keep_ref, send_ref, late_keep_ref, late_send_ref, acc_ref, dense_ref, rows_ref):
    value_width = g_ref.shape[1]
    cross_rows = n_cross * BLOCK
    my_half = want_ref[blocks_here, 0]
    far_rows = n_far * BLOCK

    def start():
        place_slots(keys_ref, rows_ref, want_ref, 0, mine_ref, other_ref, 0, my_half)
        keys_ref[:, cross_rows:, :] = early_keys_ref[...]
        if steps > 1:
            acc_ref[...] = jnp.zeros_like(acc_ref)

    def window(tile):
        b, local, _ = tile
        return n_far + b + 1, slice(local, local + tile_rows)

    def products(tile):
        here = window(tile)[1]
        keys = keys_ref[tile[0], :cross_rows, :]
        scores = dot(keys, q_ref[here, :], NT)
        grad_weights = dot(keys[:, :value_width], g_ref[here, :], NT)
        return scores, grad_weights

    def finish(tile, scores, grad_weights):
        b, _, at = tile
        slots, here = window(tile)
        early = slots * BLOCK - cross_rows
        token = lax.div(at, heads) + lax.div(lax.broadcasted_iota(jnp.int32, (BLOCK, tile_rows), 1), heads)
        place = lax.broadcasted_iota(jnp.int32, (BLOCK, tile_rows), 0)
        last = jnp.where(place <= token, early_scores_ref[early - BLOCK : early, here], MASKED)
        pieces = [
            (0, cross_rows, scores, grad_weights),
            (
                cross_rows,
                early - BLOCK,
                early_scores_ref[: early - BLOCK, here],
                early_gw_ref[: early - BLOCK, here],
            ),
            (cross_rows + early - BLOCK, BLOCK, last, early_gw_ref[early - BLOCK : early, here]),
        ]
        pieces = [
            (first, count, s.reshape(-1, BLOCK, tile_rows), gw) for first, count, s, gw in pieces if count
        ]
        biases = [bias_ref[first // BLOCK : (first + count) // BLOCK, here] for first, count, _, _ in pieces]
        tops = [
            jnp.max(jnp.max(s, axis=1) * EXP2_SCALE + bias, axis=0, keepdims=True)
            for (_, _, s, _), bias in zip(pieces, biases)
        ]
        top = functools.reduce(jnp.maximum, tops)
        raised = [
            jnp.exp2(s * EXP2_SCALE + (bias - top)[:, None, :]).reshape(-1, tile_rows)
            for (_, _, s, _), bias in zip(pieces, biases)
        ]
        total = sum(jnp.sum(r, axis=0, keepdims=True) for r in raised)
        dots = sum(jnp.sum(r * gw, axis=0, keepdims=True) for r, (_, _, _, gw) in zip(raised, pieces))
        inverse = 1.0 / total
        row_delta = dots * inverse
        for r, (first, count, _, gw) in zip(raised, pieces):
            weights = r * inverse
            weights_ref[first : first + count, here] = weights.astype(jnp.bfloat16)
            grads_ref[first : first + count, here] = (weights * (gw - row_delta)).astype(jnp.bfloat16)

    def gather(b, here):
        query_part = dot(grads_ref[:far_rows, here], q_ref[here, :], NN) * softmax_scale
        grad_part = dot(weights_ref[:far_rows, here], g_ref[here, :], NN)
        if steps == 1:
            acc_ref[b, :, :] = query_part
        else:
            acc_ref[b, :, :] += query_part
        acc_ref[b, :, :value_width] += grad_part

    def run(tiles):
        ready = products(tiles[0])
        for i, tile in enumerate(tiles):
            last = i + 1 == len(tiles)
            coming = None if last else products(tiles[i + 1])
            finish(tile, *ready)
            ready = coming
            b, local, _ = tile
            if last or tiles[i + 1][0] != b:
                first = min(t[1] for t in tiles if t[0] == b)
                gather(b, slice(first, local + tile_rows))

    def end():
        spread_slots(dense_ref, acc_ref, want_ref, range(n_far))
        write_halves(dense_ref, 0, my_half, keep_ref, send_ref)
        write_halves(dense_ref, n_cross, my_half, late_keep_ref, late_send_ref)

    at_step(0, steps, start)
    each_tile(blocks_here, heads, tile_rows, steps, run)
    at_step(steps - 1, steps, end)


def grad_kernel(n_far, blocks_here, heads, want_ref, q_ref, g_ref, weights_ref, grads_ref, keep_ref, send_ref, acc_ref, dense_ref):
    value_width = g_ref.shape[1]
    start = n_far * BLOCK
    block_rows = BLOCK * heads
    for b in range(blocks_here):
        count = (b + 1) * BLOCK
        here = slice(b * block_rows, (b + 1) * block_rows)
        acc_ref[b, :count, :] = dot(grads_ref[start : start + count, here], q_ref[here, :], NN) * softmax_scale
        acc_ref[b, :count, :value_width] += dot(weights_ref[start : start + count, here], g_ref[here, :], NN)
    for j in range(blocks_here):
        rows = slice(j * BLOCK, (j + 1) * BLOCK)
        part = acc_ref[j, rows, :]
        for b in range(j + 1, blocks_here):
            part = part + acc_ref[b, rows, :]
        dense_ref[0, rows, :] = part
    write_halves(dense_ref, 0, want_ref[blocks_here, 0], keep_ref, send_ref)


def out_kernel(n_far, blocks_here, heads, keys_ref, weights_ref, grads_ref, att_ref, gq_ref):
    tile_rows, value_width = att_ref.shape

    def tile(b):
        count = (n_far + b + 1) * BLOCK
        att_ref[...] = dot(weights_ref[:count, :], keys_ref[b, :count, :value_width], TN).astype(att_ref.dtype)
        product = dot(grads_ref[:count, :], keys_ref[b, :count, :], TN)
        gq_ref[...] = (product * softmax_scale).astype(gq_ref.dtype)

    per_block(blocks_here, tile_rows, heads, tile)


def whole(shape):
    return pl.BlockSpec(shape, lambda i: (0,) * len(shape))


def rows_of(tile_rows, width):
    return pl.BlockSpec((tile_rows, width), lambda i: (i, 0))


def lanes_of(count, tile_rows):
    return pl.BlockSpec((count, tile_rows), lambda i: (0, i))


def call(kernel, grid, in_specs, out_specs, out_shape, scratch, macs, moved, name):
    return pl.pallas_call(
        kernel,
        grid=(grid,),
        in_specs=in_specs,
        out_specs=out_specs,
        out_shape=out_shape,
        scratch_shapes=scratch,
        compiler_params=pltpu.CompilerParams(vmem_limit_bytes=VMEM_BYTES),
        cost_estimate=pl.CostEstimate(flops=2 * macs, bytes_accessed=moved, transcendentals=0),
        name=name,
    )


def whole_call(kernel, in_specs, out_specs, out_shape, scratch, macs, moved, name, steps=1):
    in_vmem = pl.BlockSpec(memory_space=pltpu.VMEM)
    if steps == 1:
        in_specs, out_specs, grid = [in_vmem] * len(in_specs), (in_vmem,) * len(out_specs), {}
    else:
        grid = {"grid": (steps,)}
    return pl.pallas_call(
        kernel,
        in_specs=[pl.BlockSpec(memory_space=pltpu.SMEM)] + list(in_specs),
        out_specs=tuple(out_specs),
        out_shape=out_shape,
        scratch_shapes=scratch,
        compiler_params=pltpu.CompilerParams(
            vmem_limit_bytes=VMEM_BYTES if steps == 1 else WIDE_BYTES
        ),
        cost_estimate=pl.CostEstimate(flops=2 * macs, bytes_accessed=moved, transcendentals=0),
        name=name,
        **grid,
    )


def tiling(rows, keys, heads):
    if rows * keys <= UNROLLED:
        return min(SCORE_ROWS, BLOCK * heads), 1
    tile_rows = min(WIDE_ROWS, BLOCK * heads)
    return tile_rows, rows // tile_rows


def table_call(place, chosen, n_far, heads):
    tok_rows = chosen.shape[1]
    blocks_here = tok_rows // BLOCK
    smem = pl.BlockSpec(memory_space=pltpu.SMEM)
    in_vmem = pl.BlockSpec(memory_space=pltpu.VMEM)
    return pl.pallas_call(
        functools.partial(table_kernel, n_far, heads),
        in_specs=[smem, in_vmem],
        out_specs=(in_vmem, smem),
        out_shape=(
            jax.ShapeDtypeStruct((n_far + blocks_here, tok_rows * heads), jnp.float32),
            jax.ShapeDtypeStruct((blocks_here + 1, n_far), jnp.int32),
        ),
        compiler_params=pltpu.CompilerParams(vmem_limit_bytes=VMEM_BYTES),
        name="table",
    )(place, chosen)


def join_call(pieces):
    in_vmem = pl.BlockSpec(memory_space=pltpu.VMEM)
    return pl.pallas_call(
        join_kernel,
        in_specs=[in_vmem] * len(pieces),
        out_specs=in_vmem,
        out_shape=jax.ShapeDtypeStruct((len(pieces),) + pieces[0].shape[1:], pieces[0].dtype),
        compiler_params=pltpu.CompilerParams(vmem_limit_bytes=VMEM_BYTES),
        name="join",
    )(*pieces)


def early_call(want, query_rows, grad_rows, own, mine, other, n_cross, n_far, heads):
    rows, width = query_rows.shape
    value_width = grad_rows.shape[1]
    tok_rows = own.shape[1]
    blocks_here = tok_rows // BLOCK
    keys = (mine.shape[0] - 1) * BLOCK + tok_rows
    tile_rows, steps = tiling(rows, n_far * BLOCK + tok_rows, heads)
    key_shape = (blocks_here, keys, width)
    by_row = [rows_of(tile_rows, width), rows_of(tile_rows, value_width)]
    return whole_call(
        functools.partial(early_kernel, n_cross, blocks_here, heads, tile_rows, steps),
        by_row + [whole(own.shape), whole(mine.shape), whole(other.shape)],
        [whole(key_shape), lanes_of(keys, tile_rows), lanes_of(keys, tile_rows), by_row[1]],
        (
            jax.ShapeDtypeStruct(key_shape, jnp.bfloat16),
            jax.ShapeDtypeStruct((keys, rows), jnp.float32),
            jax.ShapeDtypeStruct((keys, rows), jnp.float32),
            jax.ShapeDtypeStruct((rows, value_width), jnp.bfloat16),
        ),
        [pltpu.VMEM((mine.shape[0] - 1, tok_rows, width), jnp.bfloat16)],
        rows * keys * (width + value_width),
        rows * (width + value_width) * 4,
        "early_scores",
        steps,
    )(want, query_rows, grad_rows, own, mine, other)


def score_call(want, query_rows, grad_rows, bias, early, mine, other, n_far, heads, tok_rows):
    rows, width = query_rows.shape
    value_width = grad_rows.shape[1]
    blocks_here = tok_rows // BLOCK
    n_cross = mine.shape[0]
    keys = n_far * BLOCK + tok_rows
    tile_rows, steps = tiling(rows, keys, heads)
    now = jax.ShapeDtypeStruct((n_cross, width // 2, tok_rows), jnp.bfloat16)
    late = jax.ShapeDtypeStruct((n_far - n_cross, width // 2, tok_rows), jnp.bfloat16)
    early_keys = early[0].shape[1]
    key_shape = (blocks_here, keys, width)
    return whole_call(
        functools.partial(score_kernel, n_far, n_cross, blocks_here, heads, tile_rows, steps),
        [
            rows_of(tile_rows, width),
            rows_of(tile_rows, value_width),
            lanes_of(bias.shape[0], tile_rows),
            whole(early[0].shape),
            lanes_of(early_keys, tile_rows),
            lanes_of(early_keys, tile_rows),
            whole(mine.shape),
            whole(other.shape),
        ],
        [lanes_of(keys, tile_rows), lanes_of(keys, tile_rows), whole(key_shape)]
        + [whole(s.shape) for s in (now, now, late, late)],
        (
            jax.ShapeDtypeStruct((keys, rows), jnp.bfloat16),
            jax.ShapeDtypeStruct((keys, rows), jnp.bfloat16),
            jax.ShapeDtypeStruct(key_shape, jnp.bfloat16),
            now,
            now,
            late,
            late,
        ),
        [
            pltpu.VMEM((blocks_here, n_far * BLOCK, width), jnp.float32),
            pltpu.VMEM((n_far, tok_rows, width), jnp.float32),
            pltpu.VMEM((n_cross, tok_rows, width), jnp.bfloat16),
        ],
        rows * keys * 2 * (width + value_width),
        rows * (width + value_width) * 4,
        "scores",
        steps,
    )(want, query_rows, grad_rows, bias, *early, mine, other)


def grad_call(want, query_rows, grad_rows, weights, grads, n_far, heads, tok_rows):
    rows, width = query_rows.shape
    value_width = grad_rows.shape[1]
    blocks_here = tok_rows // BLOCK
    half = jax.ShapeDtypeStruct((1, width // 2, tok_rows), jnp.bfloat16)
    return whole_call(
        functools.partial(grad_kernel, n_far, blocks_here, heads),
        [None] * 4,
        [None] * 2,
        (half, half),
        [
            pltpu.VMEM((blocks_here, tok_rows, width), jnp.float32),
            pltpu.VMEM((1, tok_rows, width), jnp.float32),
        ],
        rows * tok_rows * (width + value_width),
        rows * (width + value_width) * 4,
        "own_grads",
    )(want, query_rows, grad_rows, weights, grads)


def out_call(keys, weights, grads, n_far, heads, value_width):
    blocks_here, count, width = keys.shape
    rows = weights.shape[1]
    tile_rows = min(OUT_ROWS if rows * count <= UNROLLED else WIDE_ROWS, BLOCK * heads)
    return call(
        functools.partial(out_kernel, n_far, blocks_here, heads),
        rows // tile_rows,
        [whole(keys.shape), lanes_of(count, tile_rows), lanes_of(count, tile_rows)],
        (rows_of(tile_rows, value_width), rows_of(tile_rows, width)),
        (
            jax.ShapeDtypeStruct((rows, value_width), jnp.bfloat16),
            jax.ShapeDtypeStruct((rows, width), jnp.bfloat16),
        ),
        [],
        rows * count * (width + value_width),
        rows * (width + value_width) * 4,
        "outputs",
    )(keys, weights, grads)


def body(queries, latent, cotangent, selection):
    tok_rows, heads, width = queries.shape
    value_width = cotangent.shape[2]
    shards = lax.axis_size("ctx")
    groups = lax.axis_size("head")
    my_shard = lax.axis_index("ctx")
    my_half = lax.axis_index("head") % 2
    blocks_here = tok_rows // BLOCK
    half = width // 2
    lines = shards // 2
    partner = [(i, i ^ 1) for i in range(groups)]
    across = [(i, i ^ 1) for i in range(shards)]

    def swap(rows):
        return lax.ppermute(rows, "head", partner)

    def up(rows, hops):
        return lax.ppermute(rows, "ctx", [(i, i + 2 * hops) for i in range(shards - 2 * hops)])

    def down(rows, hops):
        return lax.ppermute(rows, "ctx", [(i + 2 * hops, i) for i in range(shards - 2 * hops)])

    offsets = sorted(range(1, lines), key=lambda k: (k != 2, k))
    cross_target = (my_shard ^ 1) - 2 * jnp.array([0] + offsets, jnp.int32)
    direct_target = my_shard - 2 * jnp.array(offsets, jnp.int32)
    n_cross, n_far = lines, shards - 1
    place = jnp.concatenate(
        [jnp.stack([my_shard, my_half]).astype(jnp.int32), cross_target, direct_target]
    )
    grad_rows = cotangent.reshape(tok_rows * heads, value_width)

    turned = latent.T
    held = lax.dynamic_slice_in_dim(turned, my_half * half, half, 0)[None]
    pieces = [held] + [up(held, k) for k in offsets]
    bias, want = table_call(place, selection.T, n_far, heads)
    *pieces, bias, want, queries = lax.optimization_barrier((*pieces, bias, want, queries))
    mine = join_call(pieces)
    mine, queries = lax.optimization_barrier((mine, queries))
    cross = lax.ppermute(mine, "ctx", across)
    query_rows = queries.reshape(tok_rows * heads, width)
    *early, grad_rows = early_call(
        want, query_rows, grad_rows, turned, mine, swap(mine), n_cross, n_far, heads
    )
    cross, early[1] = lax.optimization_barrier((cross, early[1]))
    weights, grads, keys, keep, send, late_keep, late_send = score_call(
        want, query_rows, grad_rows, bias, early, cross, swap(cross), n_far, heads, tok_rows
    )

    moving = (keep.astype(jnp.float32) + swap(send).astype(jnp.float32)).astype(jnp.bfloat16)
    moving, weights, late_send = lax.optimization_barrier((moving, weights, late_send))
    arrived = lax.ppermute(moving, "ctx", across).astype(jnp.float32)
    late_send, weights = lax.optimization_barrier((swap(late_send), weights))
    own_keep, own_send = grad_call(want, query_rows, grad_rows, weights, grads, n_far, heads, tok_rows)
    own_send, weights = lax.optimization_barrier((own_send, weights))
    late = late_keep.astype(jnp.float32) + late_send.astype(jnp.float32)
    own = own_keep.astype(jnp.float32) + swap(own_send).astype(jnp.float32)
    attended, grad_queries = out_call(keys, weights, grads, n_far, heads, value_width)
    leaving = [(late[i] + arrived[i + 1]).astype(jnp.bfloat16) for i in range(n_far - n_cross)]
    total = own[0] + arrived[0]
    *leaving, total, grad_queries = lax.optimization_barrier((*leaving, total, grad_queries))
    grad_queries = grad_queries.reshape(tok_rows, heads, width).transpose(1, 2, 0)
    for part in [down(rows, k) for rows, k in zip(leaving, offsets)]:
        total = total + part.astype(jnp.float32)
    low = total.astype(jnp.bfloat16)
    low, grad_queries = lax.optimization_barrier((low, grad_queries))
    summed = low.astype(jnp.float32)
    for j in range(1, groups // 2):
        moved = lax.ppermute(low, "head", [(i, (i + 2 * j) % groups) for i in range(groups)])
        summed = summed + moved.astype(jnp.float32)
    rest = swap(summed)
    grad_latent = jnp.where(
        my_half == 0,
        jnp.concatenate([summed, rest], axis=0),
        jnp.concatenate([rest, summed], axis=0),
    )
    return (
        attended.reshape(tok_rows, heads, value_width),
        grad_queries.transpose(2, 0, 1),
        grad_latent.T,
    )


def solution(mesh):
    placed = (P("ctx", "head", None), P("ctx", None), P("ctx", "head", None), P("ctx", None))
    return jax.shard_map(
        body,
        mesh=mesh,
        in_specs=placed,
        out_specs=(P("ctx", "head", None), P("ctx", "head", None), P("ctx", None)),
        check_vma=False,
    )
```

```python
import functools

import jax
import jax.numpy as jnp
from jax import lax
from jax.experimental import pallas as pl
from jax.experimental.pallas import tpu as pltpu
from jax.sharding import PartitionSpec as P

BLOCK = 64
SCORE_ROWS = 512
OUT_ROWS = 1024
MASKED = -1e30
WIDE_ROWS = 256
VMEM_BYTES = 32 * 1024 * 1024
WIDE_BYTES = 60 * 1024 * 1024
UNROLLED = 1 << 21

softmax_scale = 192.0 ** (-0.5)
EXP2_SCALE = softmax_scale * 1.4426950408889634

NN = (((1,), (0,)), ((), ()))
NT = (((1,), (1,)), ((), ()))
TN = (((0,), (0,)), ((), ()))


def dot(a, b, dims):
    return lax.dot_general(a, b, dims, preferred_element_type=jnp.float32)


def per_block(blocks_here, tile_rows, heads, tile):
    which = lax.div(pl.program_id(0), BLOCK * heads // tile_rows)
    for b in range(blocks_here):
        pl.when(which == b)(functools.partial(tile, b))


def spread_slots(dense_ref, acc_ref, want_ref, first, count):
    dense_ref[...] = jnp.zeros_like(dense_ref)
    for b in range(acc_ref.shape[0]):
        for at in range(count):
            offset = pl.multiple_of(want_ref[b, first + at] * BLOCK, BLOCK)
            dense_ref[at, pl.ds(offset, BLOCK), :] += acc_ref[b, at * BLOCK : (at + 1) * BLOCK, :]


def write_halves(dense_ref, at, my_half, keep_ref, send_ref):
    half = keep_ref.shape[1]
    for i in range(keep_ref.shape[0]):
        turned = dense_ref[at + i, :, :].astype(keep_ref.dtype).T
        first, second = turned[:half, :], turned[half:, :]
        keep_ref[i, :, :] = jnp.where(my_half == 0, first, second)
        send_ref[i, :, :] = jnp.where(my_half == 0, second, first)


def table_kernel(n_far, heads, place_ref, chosen_ref, bias_ref, want_ref):
    tok_rows = chosen_ref.shape[1]
    blocks_here = tok_rows // BLOCK
    my_shard = place_ref[0]
    chosen = chosen_ref[...]
    valid = chosen >= 0
    owner = jnp.where(valid, lax.div(chosen, blocks_here), -1)
    inside = chosen - owner * blocks_here
    allowed = []
    for slot in range(n_far):
        target = place_ref[2 + slot]
        hit = (owner == target) & valid & (target != my_shard)
        allowed.append(jnp.max(hit.astype(jnp.float32), axis=0, keepdims=True))
        want = jnp.max(jnp.where(hit, inside, 0), axis=0, keepdims=True)
        for b in range(blocks_here):
            want_ref[b, slot] = jnp.max(want[:, b * BLOCK : (b + 1) * BLOCK])
        want_ref[blocks_here, slot] = place_ref[1]
    for j in range(blocks_here):
        hit = valid & (chosen == my_shard * blocks_here + j)
        allowed.append(jnp.max(hit.astype(jnp.float32), axis=0, keepdims=True))
    rows = tok_rows * heads
    token = lax.div(lax.broadcasted_iota(jnp.int32, (tok_rows, rows), 1), heads)
    spread = token == lax.broadcasted_iota(jnp.int32, (tok_rows, rows), 0)
    allowed = jnp.concatenate(allowed, axis=0).astype(jnp.bfloat16)
    by_row = dot(allowed, jnp.where(spread, 1.0, 0.0).astype(jnp.bfloat16), NN)
    bias_ref[...] = jnp.where(by_row > 0.5, 0.0, MASKED)


def join_kernel(*refs):
    out_ref = refs[-1]
    for i, ref in enumerate(refs[:-1]):
        out_ref[i : i + 1, :, :] = ref[...]


def place_slots(keys_ref, rows_ref, want_ref, first_slot, mine_ref, other_ref, skip, my_half):
    for slot in range(mine_ref.shape[0] - skip):
        mine, other = mine_ref[skip + slot, :, :], other_ref[skip + slot, :, :]
        turned = jnp.concatenate(
            [jnp.where(my_half == 0, mine, other), jnp.where(my_half == 0, other, mine)], axis=0
        )
        rows_ref[slot, :, :] = turned.T
        for b in range(keys_ref.shape[0]):
            offset = pl.multiple_of(want_ref[b, first_slot + slot] * BLOCK, BLOCK)
            keys_ref[b, slot * BLOCK : (slot + 1) * BLOCK, :] = rows_ref[slot, pl.ds(offset, BLOCK), :]


def each_tile(blocks_here, heads, tile_rows, steps, run):
    block_rows = BLOCK * heads
    if steps == 1:
        run([(b, b * block_rows + at, at) for b in range(blocks_here) for at in range(0, block_rows, tile_rows)])
        return
    step = pl.program_id(0)
    at = lax.rem(step, block_rows // tile_rows) * tile_rows
    for b in range(blocks_here):
        pl.when(lax.div(step, block_rows // tile_rows) == b)(functools.partial(run, [(b, 0, at)]))


def early_kernel(n_cross, blocks_here, heads, tile_rows, steps, want_ref, q_ref, g_ref, own_ref, mine_ref, other_ref, keys_ref, scores_ref, gw_ref, grad_ref, rows_ref):
    value_width = g_ref.shape[1]
    n_direct = mine_ref.shape[0] - 1

    def start():
        place_slots(keys_ref, rows_ref, want_ref, n_cross, mine_ref, other_ref, 1, want_ref[blocks_here, 0])
        own = own_ref[...].T
        for b in range(blocks_here):
            keys_ref[b, n_direct * BLOCK :, :] = own

    def run(tiles):
        for b, local, _ in tiles:
            count = (n_direct + b + 1) * BLOCK
            here = slice(local, local + tile_rows)
            scores_ref[:count, here] = dot(keys_ref[b, :count, :], q_ref[here, :], NT)
            gw_ref[:count, here] = dot(keys_ref[b, :count, :value_width], g_ref[here, :], NT)

    at_step(0, steps, start)
    grad_ref[...] = g_ref[...]
    each_tile(blocks_here, heads, tile_rows, steps, run)


def at_step(which, steps, fn):
    if steps == 1:
        fn()
    else:
        pl.when(pl.program_id(0) == which)(fn)


def score_kernel(n_far, n_cross, blocks_here, heads, tile_rows, steps, want_ref, q_ref, g_ref, bias_ref, early_keys_ref, early_scores_ref, early_gw_ref, mine_ref, other_ref, weights_ref, grads_ref, keys_ref, keep_ref, send_ref, late_keep_ref, late_send_ref, acc_ref, dense_ref, rows_ref):
    value_width = g_ref.shape[1]
    cross_rows = n_cross * BLOCK
    my_half = want_ref[blocks_here, 0]
    now_rows = (n_cross + 1) * BLOCK

    def start():
        place_slots(keys_ref, rows_ref, want_ref, 0, mine_ref, other_ref, 0, my_half)
        keys_ref[:, cross_rows:, :] = early_keys_ref[...]
        if steps > 1:
            acc_ref[...] = jnp.zeros_like(acc_ref)

    def window(tile):
        b, local, _ = tile
        return n_far + b + 1, slice(local, local + tile_rows)

    def products(tile):
        here = window(tile)[1]
        keys = keys_ref[tile[0], :cross_rows, :]
        scores = dot(keys, q_ref[here, :], NT)
        grad_weights = dot(keys[:, :value_width], g_ref[here, :], NT)
        return scores, grad_weights

    def finish(tile, scores, grad_weights):
        b, _, at = tile
        slots, here = window(tile)
        early = slots * BLOCK - cross_rows
        token = lax.div(at, heads) + lax.div(lax.broadcasted_iota(jnp.int32, (BLOCK, tile_rows), 1), heads)
        place = lax.broadcasted_iota(jnp.int32, (BLOCK, tile_rows), 0)
        last = jnp.where(place <= token, early_scores_ref[early - BLOCK : early, here], MASKED)
        pieces = [
            (0, cross_rows, scores, grad_weights),
            (
                cross_rows,
                early - BLOCK,
                early_scores_ref[: early - BLOCK, here],
                early_gw_ref[: early - BLOCK, here],
            ),
            (cross_rows + early - BLOCK, BLOCK, last, early_gw_ref[early - BLOCK : early, here]),
        ]
        pieces = [
            (first, count, s.reshape(-1, BLOCK, tile_rows), gw) for first, count, s, gw in pieces if count
        ]
        biases = [bias_ref[first // BLOCK : (first + count) // BLOCK, here] for first, count, _, _ in pieces]
        tops = [
            jnp.max(jnp.max(s, axis=1) * EXP2_SCALE + bias, axis=0, keepdims=True)
            for (_, _, s, _), bias in zip(pieces, biases)
        ]
        top = functools.reduce(jnp.maximum, tops)
        raised = [
            jnp.exp2(s * EXP2_SCALE + (bias - top)[:, None, :]).reshape(-1, tile_rows)
            for (_, _, s, _), bias in zip(pieces, biases)
        ]
        total = sum(jnp.sum(r, axis=0, keepdims=True) for r in raised)
        dots = sum(jnp.sum(r * gw, axis=0, keepdims=True) for r, (_, _, _, gw) in zip(raised, pieces))
        inverse = 1.0 / total
        row_delta = dots * inverse
        for r, (first, count, _, gw) in zip(raised, pieces):
            weights = r * inverse
            weights_ref[first : first + count, here] = weights.astype(jnp.bfloat16)
            grads_ref[first : first + count, here] = (weights * (gw - row_delta)).astype(jnp.bfloat16)

    def gather(b, here):
        query_part = dot(grads_ref[:now_rows, here], q_ref[here, :], NN) * softmax_scale
        grad_part = dot(weights_ref[:now_rows, here], g_ref[here, :], NN)
        if steps == 1:
            acc_ref[b, :, :] = query_part
        else:
            acc_ref[b, :, :] += query_part
        acc_ref[b, :, :value_width] += grad_part

    def run(tiles):
        ready = products(tiles[0])
        for i, tile in enumerate(tiles):
            last = i + 1 == len(tiles)
            coming = None if last else products(tiles[i + 1])
            finish(tile, *ready)
            ready = coming
            b, local, _ = tile
            if last or tiles[i + 1][0] != b:
                first = min(t[1] for t in tiles if t[0] == b)
                gather(b, slice(first, local + tile_rows))

    def end():
        spread_slots(dense_ref, acc_ref, want_ref, 0, n_cross + 1)
        write_halves(dense_ref, 0, my_half, keep_ref, send_ref)
        write_halves(dense_ref, n_cross, my_half, late_keep_ref, late_send_ref)

    at_step(0, steps, start)
    each_tile(blocks_here, heads, tile_rows, steps, run)
    at_step(steps - 1, steps, end)


def grad_kernel(n_far, n_now, blocks_here, heads, want_ref, q_ref, g_ref, weights_ref, grads_ref, keep_ref, send_ref, acc_ref, dense_ref):
    value_width = g_ref.shape[1]
    start = n_now * BLOCK
    n_rest = n_far - n_now
    block_rows = BLOCK * heads
    for b in range(blocks_here):
        count = (n_rest + b + 1) * BLOCK
        here = slice(b * block_rows, (b + 1) * block_rows)
        acc_ref[b, :count, :] = dot(grads_ref[start : start + count, here], q_ref[here, :], NN) * softmax_scale
        acc_ref[b, :count, :value_width] += dot(weights_ref[start : start + count, here], g_ref[here, :], NN)
    spread_slots(dense_ref, acc_ref, want_ref, n_now, n_rest)
    for j in range(blocks_here):
        at = (n_rest + j) * BLOCK
        part = acc_ref[j, at : at + BLOCK, :]
        for b in range(j + 1, blocks_here):
            part = part + acc_ref[b, at : at + BLOCK, :]
        dense_ref[n_rest, j * BLOCK : (j + 1) * BLOCK, :] = part
    write_halves(dense_ref, 0, want_ref[blocks_here, 0], keep_ref, send_ref)


def out_kernel(n_far, blocks_here, heads, keys_ref, weights_ref, grads_ref, att_ref, gq_ref):
    tile_rows, value_width = att_ref.shape

    def tile(b):
        count = (n_far + b + 1) * BLOCK
        att_ref[...] = dot(weights_ref[:count, :], keys_ref[b, :count, :value_width], TN).astype(att_ref.dtype)
        product = dot(grads_ref[:count, :], keys_ref[b, :count, :], TN)
        gq_ref[...] = (product * softmax_scale).astype(gq_ref.dtype)

    per_block(blocks_here, tile_rows, heads, tile)


def whole(shape):
    return pl.BlockSpec(shape, lambda i: (0,) * len(shape))


def rows_of(tile_rows, width):
    return pl.BlockSpec((tile_rows, width), lambda i: (i, 0))


def lanes_of(count, tile_rows):
    return pl.BlockSpec((count, tile_rows), lambda i: (0, i))


def call(kernel, grid, in_specs, out_specs, out_shape, scratch, macs, moved, name):
    return pl.pallas_call(
        kernel,
        grid=(grid,),
        in_specs=in_specs,
        out_specs=out_specs,
        out_shape=out_shape,
        scratch_shapes=scratch,
        compiler_params=pltpu.CompilerParams(vmem_limit_bytes=VMEM_BYTES),
        cost_estimate=pl.CostEstimate(flops=2 * macs, bytes_accessed=moved, transcendentals=0),
        name=name,
    )


def whole_call(kernel, in_specs, out_specs, out_shape, scratch, macs, moved, name, steps=1, wide=False):
    in_vmem = pl.BlockSpec(memory_space=pltpu.VMEM)
    if steps == 1:
        in_specs, out_specs, grid = [in_vmem] * len(in_specs), (in_vmem,) * len(out_specs), {}
    else:
        grid = {"grid": (steps,)}
    return pl.pallas_call(
        kernel,
        in_specs=[pl.BlockSpec(memory_space=pltpu.SMEM)] + list(in_specs),
        out_specs=tuple(out_specs),
        out_shape=out_shape,
        scratch_shapes=scratch,
        compiler_params=pltpu.CompilerParams(
            vmem_limit_bytes=WIDE_BYTES if wide else VMEM_BYTES
        ),
        cost_estimate=pl.CostEstimate(flops=2 * macs, bytes_accessed=moved, transcendentals=0),
        name=name,
        **grid,
    )


def tiling(rows, keys, heads):
    if rows * keys <= UNROLLED:
        return min(SCORE_ROWS, BLOCK * heads), 1
    tile_rows = min(WIDE_ROWS, BLOCK * heads)
    return tile_rows, rows // tile_rows


def table_call(place, chosen, n_far, heads):
    tok_rows = chosen.shape[1]
    blocks_here = tok_rows // BLOCK
    smem = pl.BlockSpec(memory_space=pltpu.SMEM)
    in_vmem = pl.BlockSpec(memory_space=pltpu.VMEM)
    return pl.pallas_call(
        functools.partial(table_kernel, n_far, heads),
        in_specs=[smem, in_vmem],
        out_specs=(in_vmem, smem),
        out_shape=(
            jax.ShapeDtypeStruct((n_far + blocks_here, tok_rows * heads), jnp.float32),
            jax.ShapeDtypeStruct((blocks_here + 1, n_far), jnp.int32),
        ),
        compiler_params=pltpu.CompilerParams(vmem_limit_bytes=VMEM_BYTES),
        name="table",
    )(place, chosen)


def join_call(pieces):
    in_vmem = pl.BlockSpec(memory_space=pltpu.VMEM)
    return pl.pallas_call(
        join_kernel,
        in_specs=[in_vmem] * len(pieces),
        out_specs=in_vmem,
        out_shape=jax.ShapeDtypeStruct((len(pieces),) + pieces[0].shape[1:], pieces[0].dtype),
        compiler_params=pltpu.CompilerParams(vmem_limit_bytes=VMEM_BYTES),
        name="join",
    )(*pieces)


def early_call(want, query_rows, grad_rows, own, mine, other, n_cross, n_far, heads):
    rows, width = query_rows.shape
    value_width = grad_rows.shape[1]
    tok_rows = own.shape[1]
    blocks_here = tok_rows // BLOCK
    keys = (mine.shape[0] - 1) * BLOCK + tok_rows
    tile_rows, steps = tiling(rows, n_far * BLOCK + tok_rows, heads)
    key_shape = (blocks_here, keys, width)
    by_row = [rows_of(tile_rows, width), rows_of(tile_rows, value_width)]
    return whole_call(
        functools.partial(early_kernel, n_cross, blocks_here, heads, tile_rows, steps),
        by_row + [whole(own.shape), whole(mine.shape), whole(other.shape)],
        [whole(key_shape), lanes_of(keys, tile_rows), lanes_of(keys, tile_rows), by_row[1]],
        (
            jax.ShapeDtypeStruct(key_shape, jnp.bfloat16),
            jax.ShapeDtypeStruct((keys, rows), jnp.float32),
            jax.ShapeDtypeStruct((keys, rows), jnp.float32),
            jax.ShapeDtypeStruct((rows, value_width), jnp.bfloat16),
        ),
        [pltpu.VMEM((mine.shape[0] - 1, tok_rows, width), jnp.bfloat16)],
        rows * keys * (width + value_width),
        rows * (width + value_width) * 4,
        "early_scores",
        steps,
        steps > 1,
    )(want, query_rows, grad_rows, own, mine, other)


def score_call(want, query_rows, grad_rows, bias, early, mine, other, n_far, heads, tok_rows):
    rows, width = query_rows.shape
    value_width = grad_rows.shape[1]
    blocks_here = tok_rows // BLOCK
    n_cross = mine.shape[0]
    keys = n_far * BLOCK + tok_rows
    tile_rows, steps = tiling(rows, keys, heads)
    now = jax.ShapeDtypeStruct((n_cross, width // 2, tok_rows), jnp.bfloat16)
    late = jax.ShapeDtypeStruct((1, width // 2, tok_rows), jnp.bfloat16)
    early_keys = early[0].shape[1]
    key_shape = (blocks_here, keys, width)
    return whole_call(
        functools.partial(score_kernel, n_far, n_cross, blocks_here, heads, tile_rows, steps),
        [
            rows_of(tile_rows, width),
            rows_of(tile_rows, value_width),
            lanes_of(bias.shape[0], tile_rows),
            whole(early[0].shape),
            lanes_of(early_keys, tile_rows),
            lanes_of(early_keys, tile_rows),
            whole(mine.shape),
            whole(other.shape),
        ],
        [lanes_of(keys, tile_rows), lanes_of(keys, tile_rows), whole(key_shape)]
        + [whole(s.shape) for s in (now, now, late, late)],
        (
            jax.ShapeDtypeStruct((keys, rows), jnp.bfloat16),
            jax.ShapeDtypeStruct((keys, rows), jnp.bfloat16),
            jax.ShapeDtypeStruct(key_shape, jnp.bfloat16),
            now,
            now,
            late,
            late,
        ),
        [
            pltpu.VMEM((blocks_here, (n_cross + 1) * BLOCK, width), jnp.float32),
            pltpu.VMEM((n_cross + 1, tok_rows, width), jnp.float32),
            pltpu.VMEM((n_cross, tok_rows, width), jnp.bfloat16),
        ],
        rows * keys * 2 * (width + value_width),
        rows * (width + value_width) * 4,
        "scores",
        steps,
        steps > 1,
    )(want, query_rows, grad_rows, bias, *early, mine, other)


def grad_call(want, query_rows, grad_rows, weights, grads, n_far, n_now, heads, tok_rows):
    rows, width = query_rows.shape
    value_width = grad_rows.shape[1]
    blocks_here = tok_rows // BLOCK
    n_rest = n_far - n_now
    half = jax.ShapeDtypeStruct((n_rest + 1, width // 2, tok_rows), jnp.bfloat16)
    return whole_call(
        functools.partial(grad_kernel, n_far, n_now, blocks_here, heads),
        [None] * 4,
        [None] * 2,
        (half, half),
        [
            pltpu.VMEM((blocks_here, n_rest * BLOCK + tok_rows, width), jnp.float32),
            pltpu.VMEM((n_rest + 1, tok_rows, width), jnp.float32),
        ],
        rows * (n_rest * BLOCK + tok_rows) * (width + value_width),
        rows * (width + value_width) * 4,
        "own_grads",
        1,
        rows * weights.shape[0] > UNROLLED,
    )(want, query_rows, grad_rows, weights, grads)


def out_call(keys, weights, grads, n_far, heads, value_width):
    blocks_here, count, width = keys.shape
    rows = weights.shape[1]
    tile_rows = min(OUT_ROWS if rows * count <= UNROLLED else WIDE_ROWS, BLOCK * heads)
    return call(
        functools.partial(out_kernel, n_far, blocks_here, heads),
        rows // tile_rows,
        [whole(keys.shape), lanes_of(count, tile_rows), lanes_of(count, tile_rows)],
        (rows_of(tile_rows, value_width), rows_of(tile_rows, width)),
        (
            jax.ShapeDtypeStruct((rows, value_width), jnp.bfloat16),
            jax.ShapeDtypeStruct((rows, width), jnp.bfloat16),
        ),
        [],
        rows * count * (width + value_width),
        rows * (width + value_width) * 4,
        "outputs",
    )(keys, weights, grads)


def body(queries, latent, cotangent, selection):
    tok_rows, heads, width = queries.shape
    value_width = cotangent.shape[2]
    shards = lax.axis_size("ctx")
    groups = lax.axis_size("head")
    my_shard = lax.axis_index("ctx")
    my_half = lax.axis_index("head") % 2
    blocks_here = tok_rows // BLOCK
    half = width // 2
    lines = shards // 2
    partner = [(i, i ^ 1) for i in range(groups)]
    across = [(i, i ^ 1) for i in range(shards)]

    def swap(rows):
        return lax.ppermute(rows, "head", partner)

    def up(rows, hops):
        return lax.ppermute(rows, "ctx", [(i, i + 2 * hops) for i in range(shards - 2 * hops)])

    def down(rows, hops):
        return lax.ppermute(rows, "ctx", [(i + 2 * hops, i) for i in range(shards - 2 * hops)])

    offsets = list(range(1, lines))
    cross_target = (my_shard ^ 1) - 2 * jnp.array([0] + offsets, jnp.int32)
    direct_target = my_shard - 2 * jnp.array(offsets, jnp.int32)
    n_cross, n_far = lines, shards - 1
    place = jnp.concatenate(
        [jnp.stack([my_shard, my_half]).astype(jnp.int32), cross_target, direct_target]
    )
    grad_rows = cotangent.reshape(tok_rows * heads, value_width)

    turned = latent.T
    held = lax.dynamic_slice_in_dim(turned, my_half * half, half, 0)[None]
    pieces = [held] + [up(held, k) for k in offsets]
    bias, want = table_call(place, selection.T, n_far, heads)
    *pieces, bias, want, queries = lax.optimization_barrier((*pieces, bias, want, queries))
    mine = join_call(pieces)
    mine, queries = lax.optimization_barrier((mine, queries))
    cross = lax.ppermute(mine, "ctx", across)
    query_rows = queries.reshape(tok_rows * heads, width)
    *early, grad_rows = early_call(
        want, query_rows, grad_rows, turned, mine, swap(mine), n_cross, n_far, heads
    )
    cross, early[1] = lax.optimization_barrier((cross, early[1]))
    weights, grads, keys, keep, send, late_keep, late_send = score_call(
        want, query_rows, grad_rows, bias, early, cross, swap(cross), n_far, heads, tok_rows
    )

    moving = (keep.astype(jnp.float32) + swap(send).astype(jnp.float32)).astype(jnp.bfloat16)
    moving, weights, late_send = lax.optimization_barrier((moving, weights, late_send))
    arrived = lax.ppermute(moving, "ctx", across).astype(jnp.float32)
    late_send, weights = lax.optimization_barrier((swap(late_send), weights))
    rest_keep, rest_send = grad_call(
        want, query_rows, grad_rows, weights, grads, n_far, n_cross + 1, heads, tok_rows
    )
    rest_send, weights = lax.optimization_barrier((rest_send, weights))
    late = late_keep.astype(jnp.float32) + late_send.astype(jnp.float32)
    rest = rest_keep.astype(jnp.float32) + swap(rest_send).astype(jnp.float32)
    attended, grad_queries = out_call(keys, weights, grads, n_far, heads, value_width)
    direct = [late[0]] + [rest[i] for i in range(n_far - n_cross - 1)]
    leaving = [(mine + arrived[i + 1]).astype(jnp.bfloat16) for i, mine in enumerate(direct)]
    total = rest[n_far - n_cross - 1] + arrived[0]
    *leaving, total, grad_queries = lax.optimization_barrier((*leaving, total, grad_queries))
    grad_queries = grad_queries.reshape(tok_rows, heads, width).transpose(1, 2, 0)
    for part in [down(rows, k) for k, rows in sorted(zip(offsets, leaving), key=lambda item: -item[0])]:
        total = total + part.astype(jnp.float32)
    low = total.astype(jnp.bfloat16)
    low, grad_queries = lax.optimization_barrier((low, grad_queries))
    summed = low.astype(jnp.float32)
    for j in range(1, groups // 2):
        moved = lax.ppermute(low, "head", [(i, (i + 2 * j) % groups) for i in range(groups)])
        summed = summed + moved.astype(jnp.float32)
    rest = swap(summed)
    grad_latent = jnp.where(
        my_half == 0,
        jnp.concatenate([summed, rest], axis=0),
        jnp.concatenate([rest, summed], axis=0),
    )
    return (
        attended.reshape(tok_rows, heads, value_width),
        grad_queries.transpose(2, 0, 1),
        grad_latent.T,
    )


def solution(mesh):
    placed = (P("ctx", "head", None), P("ctx", None), P("ctx", "head", None), P("ctx", None))
    return jax.shard_map(
        body,
        mesh=mesh,
        in_specs=placed,
        out_specs=(P("ctx", "head", None), P("ctx", "head", None), P("ctx", None)),
        check_vma=False,
    )
```

```python
import functools

import jax
import jax.numpy as jnp
from jax import lax
from jax.experimental import pallas as pl
from jax.experimental.pallas import tpu as pltpu
from jax.sharding import PartitionSpec as P

BLOCK = 64
SCORE_ROWS = 256
OUT_ROWS = 1024
MASKED = -1e30
WIDE_ROWS = 256
VMEM_BYTES = 32 * 1024 * 1024
WIDE_BYTES = 60 * 1024 * 1024
UNROLLED = 1 << 21

softmax_scale = 192.0 ** (-0.5)
EXP2_SCALE = softmax_scale * 1.4426950408889634

NN = (((1,), (0,)), ((), ()))
NT = (((1,), (1,)), ((), ()))
TN = (((0,), (0,)), ((), ()))


def dot(a, b, dims):
    return lax.dot_general(a, b, dims, preferred_element_type=jnp.float32)


def per_block(blocks_here, tile_rows, heads, tile):
    which = lax.div(pl.program_id(0), BLOCK * heads // tile_rows)
    for b in range(blocks_here):
        pl.when(which == b)(functools.partial(tile, b))


def spread_slots(dense_ref, acc_ref, want_ref, first, count):
    for at in range(count):
        rows = slice(at * BLOCK, (at + 1) * BLOCK)
        for j in range(dense_ref.shape[1] // BLOCK):
            placed = 0.0
            for b in range(acc_ref.shape[0]):
                placed += jnp.where(want_ref[b, first + at] == j, acc_ref[b, rows, :], 0.0)
            dense_ref[at, j * BLOCK : (j + 1) * BLOCK, :] = placed


def write_halves(dense_ref, at, my_half, keep_ref, send_ref):
    half = keep_ref.shape[1]
    for i in range(keep_ref.shape[0]):
        turned = dense_ref[at + i, :, :].astype(keep_ref.dtype).T
        first, second = turned[:half, :], turned[half:, :]
        keep_ref[i, :, :] = jnp.where(my_half == 0, first, second)
        send_ref[i, :, :] = jnp.where(my_half == 0, second, first)


def table_kernel(n_far, heads, place_ref, chosen_ref, bias_ref, want_ref):
    tok_rows = chosen_ref.shape[1]
    blocks_here = tok_rows // BLOCK
    my_shard = place_ref[0]
    chosen = chosen_ref[...]
    valid = chosen >= 0
    owner = jnp.where(valid, lax.div(chosen, blocks_here), -1)
    inside = chosen - owner * blocks_here
    allowed = []
    for slot in range(n_far):
        target = place_ref[2 + slot]
        hit = (owner == target) & valid & (target != my_shard)
        allowed.append(jnp.max(hit.astype(jnp.float32), axis=0, keepdims=True))
        want = jnp.max(jnp.where(hit, inside, 0), axis=0, keepdims=True)
        for b in range(blocks_here):
            want_ref[b, slot] = jnp.max(want[:, b * BLOCK : (b + 1) * BLOCK])
        want_ref[blocks_here, slot] = place_ref[1]
    for j in range(blocks_here):
        hit = valid & (chosen == my_shard * blocks_here + j)
        allowed.append(jnp.max(hit.astype(jnp.float32), axis=0, keepdims=True))
    rows = tok_rows * heads
    token = lax.div(lax.broadcasted_iota(jnp.int32, (tok_rows, rows), 1), heads)
    spread = token == lax.broadcasted_iota(jnp.int32, (tok_rows, rows), 0)
    allowed = jnp.concatenate(allowed, axis=0).astype(jnp.bfloat16)
    by_row = dot(allowed, jnp.where(spread, 1.0, 0.0).astype(jnp.bfloat16), NN)
    bias_ref[...] = jnp.where(by_row > 0.5, 0.0, MASKED)


def join_kernel(*refs):
    out_ref = refs[-1]
    for i, ref in enumerate(refs[:-1]):
        out_ref[i : i + 1, :, :] = ref[...]


def place_slots(keys_ref, rows_ref, want_ref, first_slot, mine_ref, other_ref, skip, my_half):
    for slot in range(mine_ref.shape[0] - skip):
        mine, other = mine_ref[skip + slot, :, :], other_ref[skip + slot, :, :]
        turned = jnp.concatenate(
            [jnp.where(my_half == 0, mine, other), jnp.where(my_half == 0, other, mine)], axis=0
        )
        rows_ref[slot, :, :] = turned.T
        for b in range(keys_ref.shape[0]):
            offset = pl.multiple_of(want_ref[b, first_slot + slot] * BLOCK, BLOCK)
            keys_ref[b, slot * BLOCK : (slot + 1) * BLOCK, :] = rows_ref[slot, pl.ds(offset, BLOCK), :]


def each_tile(blocks_here, heads, tile_rows, steps, run):
    block_rows = BLOCK * heads
    if steps == 1:
        run([(b, b * block_rows + at, at) for b in range(blocks_here) for at in range(0, block_rows, tile_rows)])
        return
    step = pl.program_id(0)
    at = lax.rem(step, block_rows // tile_rows) * tile_rows
    for b in range(blocks_here):
        pl.when(lax.div(step, block_rows // tile_rows) == b)(functools.partial(run, [(b, 0, at)]))


def early_kernel(n_cross, blocks_here, heads, tile_rows, steps, want_ref, q_ref, g_ref, own_ref, mine_ref, other_ref, keys_ref, scores_ref, gw_ref, grad_ref, rows_ref):
    value_width = g_ref.shape[1]
    n_direct = mine_ref.shape[0] - 1

    def start():
        place_slots(keys_ref, rows_ref, want_ref, n_cross, mine_ref, other_ref, 1, want_ref[blocks_here, 0])
        own = own_ref[...].T
        for b in range(blocks_here):
            keys_ref[b, n_direct * BLOCK :, :] = own

    def run(tiles):
        for b, local, _ in tiles:
            count = (n_direct + b + 1) * BLOCK
            here = slice(local, local + tile_rows)
            scores_ref[:count, here] = dot(keys_ref[b, :count, :], q_ref[here, :], NT)
            gw_ref[:count, here] = dot(keys_ref[b, :count, :value_width], g_ref[here, :], NT)

    at_step(0, steps, start)
    grad_ref[...] = g_ref[...]
    each_tile(blocks_here, heads, tile_rows, steps, run)


def at_step(which, steps, fn):
    if steps == 1:
        fn()
    else:
        pl.when(pl.program_id(0) == which)(fn)


def score_kernel(n_far, n_cross, blocks_here, heads, tile_rows, steps, want_ref, q_ref, g_ref, bias_ref, early_keys_ref, early_scores_ref, early_gw_ref, mine_ref, other_ref, weights_ref, grads_ref, keys_ref, keep_ref, send_ref, late_keep_ref, late_send_ref, acc_ref, dense_ref, rows_ref):
    value_width = g_ref.shape[1]
    cross_rows = n_cross * BLOCK
    my_half = want_ref[blocks_here, 0]
    now_rows = (n_cross + 1) * BLOCK

    def start():
        place_slots(keys_ref, rows_ref, want_ref, 0, mine_ref, other_ref, 0, my_half)
        keys_ref[:, cross_rows:, :] = early_keys_ref[...]
        if steps > 1:
            acc_ref[...] = jnp.zeros_like(acc_ref)

    def window(tile):
        b, local, _ = tile
        return n_far + b + 1, slice(local, local + tile_rows)

    def products(tile):
        here = window(tile)[1]
        keys = keys_ref[tile[0], :cross_rows, :]
        scores = dot(keys, q_ref[here, :], NT)
        grad_weights = dot(keys[:, :value_width], g_ref[here, :], NT)
        return scores, grad_weights

    def finish(tile, scores, grad_weights):
        b, _, at = tile
        slots, here = window(tile)
        early = slots * BLOCK - cross_rows
        token = lax.div(at, heads) + lax.div(lax.broadcasted_iota(jnp.int32, (BLOCK, tile_rows), 1), heads)
        place = lax.broadcasted_iota(jnp.int32, (BLOCK, tile_rows), 0)
        last = jnp.where(place <= token, early_scores_ref[early - BLOCK : early, here], MASKED)
        pieces = [
            (0, cross_rows, scores, grad_weights),
            (
                cross_rows,
                early - BLOCK,
                early_scores_ref[: early - BLOCK, here],
                early_gw_ref[: early - BLOCK, here],
            ),
            (cross_rows + early - BLOCK, BLOCK, last, early_gw_ref[early - BLOCK : early, here]),
        ]
        pieces = [
            (first, count, s.reshape(-1, BLOCK, tile_rows), gw) for first, count, s, gw in pieces if count
        ]
        biases = [bias_ref[first // BLOCK : (first + count) // BLOCK, here] for first, count, _, _ in pieces]
        tops = [
            jnp.max(jnp.max(s, axis=1) * EXP2_SCALE + bias, axis=0, keepdims=True)
            for (_, _, s, _), bias in zip(pieces, biases)
        ]
        top = functools.reduce(jnp.maximum, tops)
        raised = [
            jnp.exp2(s * EXP2_SCALE + (bias - top)[:, None, :]).reshape(-1, tile_rows)
            for (_, _, s, _), bias in zip(pieces, biases)
        ]
        total = sum(jnp.sum(r, axis=0, keepdims=True) for r in raised)
        dots = sum(jnp.sum(r * gw, axis=0, keepdims=True) for r, (_, _, _, gw) in zip(raised, pieces))
        inverse = 1.0 / total
        row_delta = dots * inverse
        for r, (first, count, _, gw) in zip(raised, pieces):
            weights = r * inverse
            weights_ref[first : first + count, here] = weights.astype(jnp.bfloat16)
            grads_ref[first : first + count, here] = (weights * (gw - row_delta)).astype(jnp.bfloat16)

    def gather(b, here):
        query_part = dot(grads_ref[:now_rows, here], q_ref[here, :], NN) * softmax_scale
        grad_part = dot(weights_ref[:now_rows, here], g_ref[here, :], NN)
        if steps == 1:
            acc_ref[b, :, :] = query_part
        else:
            acc_ref[b, :, :] += query_part
        acc_ref[b, :, :value_width] += grad_part

    def run(tiles):
        ready = products(tiles[0])
        for i, tile in enumerate(tiles):
            last = i + 1 == len(tiles)
            coming = None if last else products(tiles[i + 1])
            finish(tile, *ready)
            ready = coming
            b, local, _ = tile
            if last or tiles[i + 1][0] != b:
                first = min(t[1] for t in tiles if t[0] == b)
                gather(b, slice(first, local + tile_rows))

    def end():
        spread_slots(dense_ref, acc_ref, want_ref, 0, n_cross + 1)
        write_halves(dense_ref, 0, my_half, keep_ref, send_ref)
        write_halves(dense_ref, n_cross, my_half, late_keep_ref, late_send_ref)

    at_step(0, steps, start)
    each_tile(blocks_here, heads, tile_rows, steps, run)
    at_step(steps - 1, steps, end)


def grad_kernel(n_far, n_now, blocks_here, heads, want_ref, q_ref, g_ref, weights_ref, grads_ref, keep_ref, send_ref, acc_ref, dense_ref):
    value_width = g_ref.shape[1]
    start = n_now * BLOCK
    n_rest = n_far - n_now
    block_rows = BLOCK * heads
    for b in range(blocks_here):
        count = (n_rest + b + 1) * BLOCK
        here = slice(b * block_rows, (b + 1) * block_rows)
        acc_ref[b, :count, :] = dot(grads_ref[start : start + count, here], q_ref[here, :], NN) * softmax_scale
        acc_ref[b, :count, :value_width] += dot(weights_ref[start : start + count, here], g_ref[here, :], NN)
    spread_slots(dense_ref, acc_ref, want_ref, n_now, n_rest)
    for j in range(blocks_here):
        at = (n_rest + j) * BLOCK
        part = acc_ref[j, at : at + BLOCK, :]
        for b in range(j + 1, blocks_here):
            part = part + acc_ref[b, at : at + BLOCK, :]
        dense_ref[n_rest, j * BLOCK : (j + 1) * BLOCK, :] = part
    write_halves(dense_ref, 0, want_ref[blocks_here, 0], keep_ref, send_ref)


def out_kernel(n_far, blocks_here, heads, keys_ref, weights_ref, grads_ref, att_ref, gq_ref):
    tile_rows, value_width = att_ref.shape

    def tile(b):
        count = (n_far + b + 1) * BLOCK
        att_ref[...] = dot(weights_ref[:count, :], keys_ref[b, :count, :value_width], TN).astype(att_ref.dtype)
        product = dot(grads_ref[:count, :], keys_ref[b, :count, :], TN)
        gq_ref[...] = (product * softmax_scale).astype(gq_ref.dtype)

    per_block(blocks_here, tile_rows, heads, tile)


def whole(shape):
    return pl.BlockSpec(shape, lambda i: (0,) * len(shape))


def rows_of(tile_rows, width):
    return pl.BlockSpec((tile_rows, width), lambda i: (i, 0))


def lanes_of(count, tile_rows):
    return pl.BlockSpec((count, tile_rows), lambda i: (0, i))


def call(kernel, grid, in_specs, out_specs, out_shape, scratch, macs, moved, name):
    return pl.pallas_call(
        kernel,
        grid=(grid,),
        in_specs=in_specs,
        out_specs=out_specs,
        out_shape=out_shape,
        scratch_shapes=scratch,
        compiler_params=pltpu.CompilerParams(vmem_limit_bytes=VMEM_BYTES),
        cost_estimate=pl.CostEstimate(flops=2 * macs, bytes_accessed=moved, transcendentals=0),
        name=name,
    )


def whole_call(kernel, in_specs, out_specs, out_shape, scratch, macs, moved, name, steps=1, wide=False):
    in_vmem = pl.BlockSpec(memory_space=pltpu.VMEM)
    if steps == 1:
        in_specs, out_specs, grid = [in_vmem] * len(in_specs), (in_vmem,) * len(out_specs), {}
    else:
        grid = {"grid": (steps,)}
    return pl.pallas_call(
        kernel,
        in_specs=[pl.BlockSpec(memory_space=pltpu.SMEM)] + list(in_specs),
        out_specs=tuple(out_specs),
        out_shape=out_shape,
        scratch_shapes=scratch,
        compiler_params=pltpu.CompilerParams(
            vmem_limit_bytes=WIDE_BYTES if wide else VMEM_BYTES
        ),
        cost_estimate=pl.CostEstimate(flops=2 * macs, bytes_accessed=moved, transcendentals=0),
        name=name,
        **grid,
    )


def tiling(rows, keys, heads):
    if rows * keys <= UNROLLED:
        return min(SCORE_ROWS, BLOCK * heads), 1
    tile_rows = min(WIDE_ROWS, BLOCK * heads)
    return tile_rows, rows // tile_rows


def table_call(place, chosen, n_far, heads):
    tok_rows = chosen.shape[1]
    blocks_here = tok_rows // BLOCK
    smem = pl.BlockSpec(memory_space=pltpu.SMEM)
    in_vmem = pl.BlockSpec(memory_space=pltpu.VMEM)
    return pl.pallas_call(
        functools.partial(table_kernel, n_far, heads),
        in_specs=[smem, in_vmem],
        out_specs=(in_vmem, smem),
        out_shape=(
            jax.ShapeDtypeStruct((n_far + blocks_here, tok_rows * heads), jnp.float32),
            jax.ShapeDtypeStruct((blocks_here + 1, n_far), jnp.int32),
        ),
        compiler_params=pltpu.CompilerParams(vmem_limit_bytes=VMEM_BYTES),
        name="table",
    )(place, chosen)


def join_call(pieces):
    in_vmem = pl.BlockSpec(memory_space=pltpu.VMEM)
    return pl.pallas_call(
        join_kernel,
        in_specs=[in_vmem] * len(pieces),
        out_specs=in_vmem,
        out_shape=jax.ShapeDtypeStruct((len(pieces),) + pieces[0].shape[1:], pieces[0].dtype),
        compiler_params=pltpu.CompilerParams(vmem_limit_bytes=VMEM_BYTES),
        name="join",
    )(*pieces)


def early_call(want, query_rows, grad_rows, own, mine, other, n_cross, n_far, heads):
    rows, width = query_rows.shape
    value_width = grad_rows.shape[1]
    tok_rows = own.shape[1]
    blocks_here = tok_rows // BLOCK
    keys = (mine.shape[0] - 1) * BLOCK + tok_rows
    tile_rows, steps = tiling(rows, n_far * BLOCK + tok_rows, heads)
    key_shape = (blocks_here, keys, width)
    by_row = [rows_of(tile_rows, width), rows_of(tile_rows, value_width)]
    return whole_call(
        functools.partial(early_kernel, n_cross, blocks_here, heads, tile_rows, steps),
        by_row + [whole(own.shape), whole(mine.shape), whole(other.shape)],
        [whole(key_shape), lanes_of(keys, tile_rows), lanes_of(keys, tile_rows), by_row[1]],
        (
            jax.ShapeDtypeStruct(key_shape, jnp.bfloat16),
            jax.ShapeDtypeStruct((keys, rows), jnp.float32),
            jax.ShapeDtypeStruct((keys, rows), jnp.float32),
            jax.ShapeDtypeStruct((rows, value_width), jnp.bfloat16),
        ),
        [pltpu.VMEM((mine.shape[0] - 1, tok_rows, width), jnp.bfloat16)],
        rows * keys * (width + value_width),
        rows * (width + value_width) * 4,
        "early_scores",
        steps,
        steps > 1,
    )(want, query_rows, grad_rows, own, mine, other)


def score_call(want, query_rows, grad_rows, bias, early, mine, other, n_far, heads, tok_rows):
    rows, width = query_rows.shape
    value_width = grad_rows.shape[1]
    blocks_here = tok_rows // BLOCK
    n_cross = mine.shape[0]
    keys = n_far * BLOCK + tok_rows
    tile_rows, steps = tiling(rows, keys, heads)
    now = jax.ShapeDtypeStruct((n_cross, width // 2, tok_rows), jnp.bfloat16)
    late = jax.ShapeDtypeStruct((1, width // 2, tok_rows), jnp.bfloat16)
    early_keys = early[0].shape[1]
    key_shape = (blocks_here, keys, width)
    return whole_call(
        functools.partial(score_kernel, n_far, n_cross, blocks_here, heads, tile_rows, steps),
        [
            rows_of(tile_rows, width),
            rows_of(tile_rows, value_width),
            lanes_of(bias.shape[0], tile_rows),
            whole(early[0].shape),
            lanes_of(early_keys, tile_rows),
            lanes_of(early_keys, tile_rows),
            whole(mine.shape),
            whole(other.shape),
        ],
        [lanes_of(keys, tile_rows), lanes_of(keys, tile_rows), whole(key_shape)]
        + [whole(s.shape) for s in (now, now, late, late)],
        (
            jax.ShapeDtypeStruct((keys, rows), jnp.bfloat16),
            jax.ShapeDtypeStruct((keys, rows), jnp.bfloat16),
            jax.ShapeDtypeStruct(key_shape, jnp.bfloat16),
            now,
            now,
            late,
            late,
        ),
        [
            pltpu.VMEM((blocks_here, (n_cross + 1) * BLOCK, width), jnp.float32),
            pltpu.VMEM((n_cross + 1, tok_rows, width), jnp.float32),
            pltpu.VMEM((n_cross, tok_rows, width), jnp.bfloat16),
        ],
        rows * keys * 2 * (width + value_width),
        rows * (width + value_width) * 4,
        "scores",
        steps,
        steps > 1,
    )(want, query_rows, grad_rows, bias, *early, mine, other)


def grad_call(want, query_rows, grad_rows, weights, grads, n_far, n_now, heads, tok_rows):
    rows, width = query_rows.shape
    value_width = grad_rows.shape[1]
    blocks_here = tok_rows // BLOCK
    n_rest = n_far - n_now
    half = jax.ShapeDtypeStruct((n_rest + 1, width // 2, tok_rows), jnp.bfloat16)
    return whole_call(
        functools.partial(grad_kernel, n_far, n_now, blocks_here, heads),
        [None] * 4,
        [None] * 2,
        (half, half),
        [
            pltpu.VMEM((blocks_here, n_rest * BLOCK + tok_rows, width), jnp.float32),
            pltpu.VMEM((n_rest + 1, tok_rows, width), jnp.float32),
        ],
        rows * (n_rest * BLOCK + tok_rows) * (width + value_width),
        rows * (width + value_width) * 4,
        "own_grads",
        1,
        rows * weights.shape[0] > UNROLLED,
    )(want, query_rows, grad_rows, weights, grads)


def out_call(keys, weights, grads, n_far, heads, value_width):
    blocks_here, count, width = keys.shape
    rows = weights.shape[1]
    tile_rows = min(OUT_ROWS if rows * count <= UNROLLED else WIDE_ROWS, BLOCK * heads)
    return call(
        functools.partial(out_kernel, n_far, blocks_here, heads),
        rows // tile_rows,
        [whole(keys.shape), lanes_of(count, tile_rows), lanes_of(count, tile_rows)],
        (rows_of(tile_rows, value_width), rows_of(tile_rows, width)),
        (
            jax.ShapeDtypeStruct((rows, value_width), jnp.bfloat16),
            jax.ShapeDtypeStruct((rows, width), jnp.bfloat16),
        ),
        [],
        rows * count * (width + value_width),
        rows * (width + value_width) * 4,
        "outputs",
    )(keys, weights, grads)


def body(queries, latent, cotangent, selection):
    tok_rows, heads, width = queries.shape
    value_width = cotangent.shape[2]
    shards = lax.axis_size("ctx")
    groups = lax.axis_size("head")
    my_shard = lax.axis_index("ctx")
    my_half = lax.axis_index("head") % 2
    blocks_here = tok_rows // BLOCK
    half = width // 2
    lines = shards // 2
    partner = [(i, i ^ 1) for i in range(groups)]
    across = [(i, i ^ 1) for i in range(shards)]

    def swap(rows):
        return lax.ppermute(rows, "head", partner)

    def up(rows, hops):
        return lax.ppermute(rows, "ctx", [(i, i + 2 * hops) for i in range(shards - 2 * hops)])

    def down(rows, hops):
        return lax.ppermute(rows, "ctx", [(i + 2 * hops, i) for i in range(shards - 2 * hops)])

    offsets = list(range(1, lines))
    cross_target = (my_shard ^ 1) - 2 * jnp.array([0] + offsets, jnp.int32)
    direct_target = my_shard - 2 * jnp.array(offsets, jnp.int32)
    n_cross, n_far = lines, shards - 1
    place = jnp.concatenate(
        [jnp.stack([my_shard, my_half]).astype(jnp.int32), cross_target, direct_target]
    )
    grad_rows = cotangent.reshape(tok_rows * heads, value_width)

    turned = latent.T
    held = lax.dynamic_slice_in_dim(turned, my_half * half, half, 0)[None]
    pieces = [held] + [up(held, k) for k in offsets]
    bias, want = table_call(place, selection.T, n_far, heads)
    *pieces, bias, want, queries = lax.optimization_barrier((*pieces, bias, want, queries))
    mine = join_call(pieces)
    mine, queries = lax.optimization_barrier((mine, queries))
    cross = lax.ppermute(mine, "ctx", across)
    query_rows = queries.reshape(tok_rows * heads, width)
    *early, grad_rows = early_call(
        want, query_rows, grad_rows, turned, mine, swap(mine), n_cross, n_far, heads
    )
    cross, early[1] = lax.optimization_barrier((cross, early[1]))
    weights, grads, keys, keep, send, late_keep, late_send = score_call(
        want, query_rows, grad_rows, bias, early, cross, swap(cross), n_far, heads, tok_rows
    )

    moving = (keep.astype(jnp.float32) + swap(send).astype(jnp.float32)).astype(jnp.bfloat16)
    moving, weights, late_send = lax.optimization_barrier((moving, weights, late_send))
    arrived = lax.ppermute(moving, "ctx", across).astype(jnp.float32)
    late_send, weights = lax.optimization_barrier((swap(late_send), weights))
    rest_keep, rest_send = grad_call(
        want, query_rows, grad_rows, weights, grads, n_far, n_cross + 1, heads, tok_rows
    )
    rest_send, weights = lax.optimization_barrier((rest_send, weights))
    late = late_keep.astype(jnp.float32) + late_send.astype(jnp.float32)
    rest = rest_keep.astype(jnp.float32) + swap(rest_send).astype(jnp.float32)
    attended, grad_queries = out_call(keys, weights, grads, n_far, heads, value_width)
    direct = [late[0]] + [rest[i] for i in range(n_far - n_cross - 1)]
    leaving = [(mine + arrived[i + 1]).astype(jnp.bfloat16) for i, mine in enumerate(direct)]
    total = rest[n_far - n_cross - 1] + arrived[0]
    *leaving, total, grad_queries = lax.optimization_barrier((*leaving, total, grad_queries))
    grad_queries = grad_queries.reshape(tok_rows, heads, width).transpose(1, 2, 0)
    for part in [down(rows, k) for k, rows in sorted(zip(offsets, leaving), key=lambda item: -item[0])]:
        total = total + part.astype(jnp.float32)
    low = total.astype(jnp.bfloat16)
    low, grad_queries = lax.optimization_barrier((low, grad_queries))
    summed = low.astype(jnp.float32)
    for j in range(1, groups // 2):
        moved = lax.ppermute(low, "head", [(i, (i + 2 * j) % groups) for i in range(groups)])
        summed = summed + moved.astype(jnp.float32)
    rest = swap(summed)
    grad_latent = jnp.where(
        my_half == 0,
        jnp.concatenate([summed, rest], axis=0),
        jnp.concatenate([rest, summed], axis=0),
    )
    return (
        attended.reshape(tok_rows, heads, value_width),
        grad_queries.transpose(2, 0, 1),
        grad_latent.T,
    )


def solution(mesh):
    placed = (P("ctx", "head", None), P("ctx", None), P("ctx", "head", None), P("ctx", None))
    return jax.shard_map(
        body,
        mesh=mesh,
        in_specs=placed,
        out_specs=(P("ctx", "head", None), P("ctx", "head", None), P("ctx", None)),
        check_vma=False,
    )
```

```python
import functools

import jax
import jax.numpy as jnp
from jax import lax
from jax.experimental import pallas as pl
from jax.experimental.pallas import tpu as pltpu
from jax.sharding import PartitionSpec as P

BLOCK = 64
SCORE_ROWS = 256
OUT_ROWS = 1024
MASKED = -1e30
WIDE_ROWS = 256
VMEM_BYTES = 20 * 1024 * 1024
WIDE_BYTES = 60 * 1024 * 1024
UNROLLED = 1 << 21

softmax_scale = 192.0 ** (-0.5)
EXP2_SCALE = softmax_scale * 1.4426950408889634

NN = (((1,), (0,)), ((), ()))
NT = (((1,), (1,)), ((), ()))
TN = (((0,), (0,)), ((), ()))


def dot(a, b, dims):
    return lax.dot_general(a, b, dims, preferred_element_type=jnp.float32)


def per_block(blocks_here, tile_rows, heads, tile):
    which = lax.div(pl.program_id(0), BLOCK * heads // tile_rows)
    for b in range(blocks_here):
        pl.when(which == b)(functools.partial(tile, b))


def spread_slots(dense_ref, acc_ref, want_ref, first, count):
    for at in range(count):
        rows = slice(at * BLOCK, (at + 1) * BLOCK)
        for j in range(dense_ref.shape[1] // BLOCK):
            placed = 0.0
            for b in range(acc_ref.shape[0]):
                placed += jnp.where(want_ref[b, first + at] == j, acc_ref[b, rows, :], 0.0)
            dense_ref[at, j * BLOCK : (j + 1) * BLOCK, :] = placed


def write_halves(dense_ref, at, my_half, keep_ref, send_ref):
    half = keep_ref.shape[1]
    for i in range(keep_ref.shape[0]):
        turned = dense_ref[at + i, :, :].astype(keep_ref.dtype).T
        first, second = turned[:half, :], turned[half:, :]
        keep_ref[i, :, :] = jnp.where(my_half == 0, first, second)
        send_ref[i, :, :] = jnp.where(my_half == 0, second, first)


def table_kernel(n_far, heads, place_ref, chosen_ref, bias_ref, want_ref):
    tok_rows = chosen_ref.shape[1]
    blocks_here = tok_rows // BLOCK
    my_shard = place_ref[0]
    chosen = chosen_ref[...]
    valid = chosen >= 0
    owner = jnp.where(valid, lax.div(chosen, blocks_here), -1)
    inside = chosen - owner * blocks_here
    allowed = []
    for slot in range(n_far):
        target = place_ref[2 + slot]
        hit = (owner == target) & valid & (target != my_shard)
        allowed.append(jnp.max(hit.astype(jnp.float32), axis=0, keepdims=True))
        want = jnp.max(jnp.where(hit, inside, 0), axis=0, keepdims=True)
        for b in range(blocks_here):
            want_ref[b, slot] = jnp.max(want[:, b * BLOCK : (b + 1) * BLOCK])
        want_ref[blocks_here, slot] = place_ref[1]
    for j in range(blocks_here):
        hit = valid & (chosen == my_shard * blocks_here + j)
        allowed.append(jnp.max(hit.astype(jnp.float32), axis=0, keepdims=True))
    rows = tok_rows * heads
    token = lax.div(lax.broadcasted_iota(jnp.int32, (tok_rows, rows), 1), heads)
    spread = token == lax.broadcasted_iota(jnp.int32, (tok_rows, rows), 0)
    allowed = jnp.concatenate(allowed, axis=0).astype(jnp.bfloat16)
    by_row = dot(allowed, jnp.where(spread, 1.0, 0.0).astype(jnp.bfloat16), NN)
    bias_ref[...] = jnp.where(by_row > 0.5, 0.0, MASKED)


def join_kernel(*refs):
    out_ref = refs[-1]
    for i, ref in enumerate(refs[:-1]):
        out_ref[i : i + 1, :, :] = ref[...]


def place_slots(keys_ref, rows_ref, want_ref, first_slot, mine_ref, other_ref, skip, my_half):
    for slot in range(mine_ref.shape[0] - skip):
        mine, other = mine_ref[skip + slot, :, :], other_ref[skip + slot, :, :]
        turned = jnp.concatenate(
            [jnp.where(my_half == 0, mine, other), jnp.where(my_half == 0, other, mine)], axis=0
        )
        rows_ref[slot, :, :] = turned.T
        for b in range(keys_ref.shape[0]):
            offset = pl.multiple_of(want_ref[b, first_slot + slot] * BLOCK, BLOCK)
            keys_ref[b, slot * BLOCK : (slot + 1) * BLOCK, :] = rows_ref[slot, pl.ds(offset, BLOCK), :]


def each_tile(blocks_here, heads, tile_rows, steps, run):
    block_rows = BLOCK * heads
    if steps == 1:
        run([(b, b * block_rows + at, at) for b in range(blocks_here) for at in range(0, block_rows, tile_rows)])
        return
    step = pl.program_id(0)
    at = lax.rem(step, block_rows // tile_rows) * tile_rows
    for b in range(blocks_here):
        pl.when(lax.div(step, block_rows // tile_rows) == b)(functools.partial(run, [(b, 0, at)]))


def early_kernel(n_cross, blocks_here, heads, tile_rows, steps, want_ref, q_ref, g_ref, own_ref, mine_ref, other_ref, keys_ref, scores_ref, gw_ref, grad_ref, rows_ref):
    value_width = g_ref.shape[1]
    n_direct = mine_ref.shape[0] - 1

    def start():
        place_slots(keys_ref, rows_ref, want_ref, n_cross, mine_ref, other_ref, 1, want_ref[blocks_here, 0])
        own = own_ref[...].T
        for b in range(blocks_here):
            keys_ref[b, n_direct * BLOCK :, :] = own

    def run(tiles):
        for b, local, _ in tiles:
            count = (n_direct + b + 1) * BLOCK
            here = slice(local, local + tile_rows)
            scores_ref[:count, here] = dot(keys_ref[b, :count, :], q_ref[here, :], NT)
            gw_ref[:count, here] = dot(keys_ref[b, :count, :value_width], g_ref[here, :], NT)

    at_step(0, steps, start)
    grad_ref[...] = g_ref[...]
    each_tile(blocks_here, heads, tile_rows, steps, run)


def at_step(which, steps, fn):
    if steps == 1:
        fn()
    else:
        pl.when(pl.program_id(0) == which)(fn)


def score_kernel(n_far, n_cross, blocks_here, heads, tile_rows, steps, want_ref, q_ref, g_ref, bias_ref, early_keys_ref, early_scores_ref, early_gw_ref, mine_ref, other_ref, weights_ref, grads_ref, keys_ref, keep_ref, send_ref, late_keep_ref, late_send_ref, acc_ref, dense_ref, rows_ref):
    value_width = g_ref.shape[1]
    cross_rows = n_cross * BLOCK
    my_half = want_ref[blocks_here, 0]
    now_rows = (n_cross + 1) * BLOCK

    def start():
        place_slots(keys_ref, rows_ref, want_ref, 0, mine_ref, other_ref, 0, my_half)
        keys_ref[:, cross_rows:, :] = early_keys_ref[...]
        if steps > 1:
            acc_ref[...] = jnp.zeros_like(acc_ref)

    def window(tile):
        b, local, _ = tile
        return n_far + b + 1, slice(local, local + tile_rows)

    def products(tile):
        here = window(tile)[1]
        keys = keys_ref[tile[0], :cross_rows, :]
        scores = dot(keys, q_ref[here, :], NT)
        grad_weights = dot(keys[:, :value_width], g_ref[here, :], NT)
        return scores, grad_weights

    def finish(tile, scores, grad_weights):
        b, _, at = tile
        slots, here = window(tile)
        early = slots * BLOCK - cross_rows
        token = lax.div(at, heads) + lax.div(lax.broadcasted_iota(jnp.int32, (BLOCK, tile_rows), 1), heads)
        place = lax.broadcasted_iota(jnp.int32, (BLOCK, tile_rows), 0)
        last = jnp.where(place <= token, early_scores_ref[early - BLOCK : early, here], MASKED)
        pieces = [
            (0, cross_rows, scores, grad_weights),
            (
                cross_rows,
                early - BLOCK,
                early_scores_ref[: early - BLOCK, here],
                early_gw_ref[: early - BLOCK, here],
            ),
            (cross_rows + early - BLOCK, BLOCK, last, early_gw_ref[early - BLOCK : early, here]),
        ]
        pieces = [
            (first, count, s.reshape(-1, BLOCK, tile_rows), gw) for first, count, s, gw in pieces if count
        ]
        biases = [bias_ref[first // BLOCK : (first + count) // BLOCK, here] for first, count, _, _ in pieces]
        tops = [
            jnp.max(jnp.max(s, axis=1) * EXP2_SCALE + bias, axis=0, keepdims=True)
            for (_, _, s, _), bias in zip(pieces, biases)
        ]
        top = functools.reduce(jnp.maximum, tops)
        raised = [
            jnp.exp2(s * EXP2_SCALE + (bias - top)[:, None, :]).reshape(-1, tile_rows)
            for (_, _, s, _), bias in zip(pieces, biases)
        ]
        total = sum(jnp.sum(r, axis=0, keepdims=True) for r in raised)
        dots = sum(jnp.sum(r * gw, axis=0, keepdims=True) for r, (_, _, _, gw) in zip(raised, pieces))
        inverse = 1.0 / total
        row_delta = dots * inverse
        for r, (first, count, _, gw) in zip(raised, pieces):
            weights = r * inverse
            weights_ref[first : first + count, here] = weights.astype(jnp.bfloat16)
            grads_ref[first : first + count, here] = (weights * (gw - row_delta)).astype(jnp.bfloat16)

    def gather(b, here):
        query_part = dot(grads_ref[:now_rows, here], q_ref[here, :], NN) * softmax_scale
        grad_part = dot(weights_ref[:now_rows, here], g_ref[here, :], NN)
        if steps == 1:
            acc_ref[b, :, :] = query_part
        else:
            acc_ref[b, :, :] += query_part
        acc_ref[b, :, :value_width] += grad_part

    def run(tiles):
        ready = products(tiles[0])
        for i, tile in enumerate(tiles):
            last = i + 1 == len(tiles)
            coming = None if last else products(tiles[i + 1])
            finish(tile, *ready)
            ready = coming
            b, local, _ = tile
            if last or tiles[i + 1][0] != b:
                first = min(t[1] for t in tiles if t[0] == b)
                gather(b, slice(first, local + tile_rows))

    def end():
        spread_slots(dense_ref, acc_ref, want_ref, 0, n_cross + 1)
        write_halves(dense_ref, 0, my_half, keep_ref, send_ref)
        write_halves(dense_ref, n_cross, my_half, late_keep_ref, late_send_ref)

    at_step(0, steps, start)
    each_tile(blocks_here, heads, tile_rows, steps, run)
    at_step(steps - 1, steps, end)


def grad_kernel(n_far, n_now, blocks_here, heads, want_ref, q_ref, g_ref, weights_ref, grads_ref, keep_ref, send_ref, acc_ref, dense_ref):
    value_width = g_ref.shape[1]
    start = n_now * BLOCK
    n_rest = n_far - n_now
    block_rows = BLOCK * heads
    for b in range(blocks_here):
        count = (n_rest + b + 1) * BLOCK
        here = slice(b * block_rows, (b + 1) * block_rows)
        acc_ref[b, :count, :] = dot(grads_ref[start : start + count, here], q_ref[here, :], NN) * softmax_scale
        acc_ref[b, :count, :value_width] += dot(weights_ref[start : start + count, here], g_ref[here, :], NN)
    spread_slots(dense_ref, acc_ref, want_ref, n_now, n_rest)
    for j in range(blocks_here):
        at = (n_rest + j) * BLOCK
        part = acc_ref[j, at : at + BLOCK, :]
        for b in range(j + 1, blocks_here):
            part = part + acc_ref[b, at : at + BLOCK, :]
        dense_ref[n_rest, j * BLOCK : (j + 1) * BLOCK, :] = part
    write_halves(dense_ref, 0, want_ref[blocks_here, 0], keep_ref, send_ref)


def out_kernel(n_far, blocks_here, heads, keys_ref, weights_ref, grads_ref, att_ref, gq_ref):
    tile_rows, value_width = att_ref.shape

    def tile(b):
        count = (n_far + b + 1) * BLOCK
        att_ref[...] = dot(weights_ref[:count, :], keys_ref[b, :count, :value_width], TN).astype(att_ref.dtype)
        product = dot(grads_ref[:count, :], keys_ref[b, :count, :], TN)
        gq_ref[...] = (product * softmax_scale).astype(gq_ref.dtype)

    per_block(blocks_here, tile_rows, heads, tile)


def whole(shape):
    return pl.BlockSpec(shape, lambda i: (0,) * len(shape))


def rows_of(tile_rows, width):
    return pl.BlockSpec((tile_rows, width), lambda i: (i, 0))


def lanes_of(count, tile_rows):
    return pl.BlockSpec((count, tile_rows), lambda i: (0, i))


def call(kernel, grid, in_specs, out_specs, out_shape, scratch, macs, moved, name):
    return pl.pallas_call(
        kernel,
        grid=(grid,),
        in_specs=in_specs,
        out_specs=out_specs,
        out_shape=out_shape,
        scratch_shapes=scratch,
        compiler_params=pltpu.CompilerParams(vmem_limit_bytes=VMEM_BYTES),
        cost_estimate=pl.CostEstimate(flops=2 * macs, bytes_accessed=moved, transcendentals=0),
        name=name,
    )


def whole_call(kernel, in_specs, out_specs, out_shape, scratch, macs, moved, name, steps=1, wide=False):
    in_vmem = pl.BlockSpec(memory_space=pltpu.VMEM)
    if steps == 1:
        in_specs, out_specs, grid = [in_vmem] * len(in_specs), (in_vmem,) * len(out_specs), {}
    else:
        grid = {"grid": (steps,)}
    return pl.pallas_call(
        kernel,
        in_specs=[pl.BlockSpec(memory_space=pltpu.SMEM)] + list(in_specs),
        out_specs=tuple(out_specs),
        out_shape=out_shape,
        scratch_shapes=scratch,
        compiler_params=pltpu.CompilerParams(
            vmem_limit_bytes=WIDE_BYTES if wide else VMEM_BYTES
        ),
        cost_estimate=pl.CostEstimate(flops=2 * macs, bytes_accessed=moved, transcendentals=0),
        name=name,
        **grid,
    )


def tiling(rows, keys, heads):
    if rows * keys <= UNROLLED:
        return min(SCORE_ROWS, BLOCK * heads), 1
    tile_rows = min(WIDE_ROWS, BLOCK * heads)
    return tile_rows, rows // tile_rows


def table_call(place, chosen, n_far, heads):
    tok_rows = chosen.shape[1]
    blocks_here = tok_rows // BLOCK
    smem = pl.BlockSpec(memory_space=pltpu.SMEM)
    in_vmem = pl.BlockSpec(memory_space=pltpu.VMEM)
    return pl.pallas_call(
        functools.partial(table_kernel, n_far, heads),
        in_specs=[smem, in_vmem],
        out_specs=(in_vmem, smem),
        out_shape=(
            jax.ShapeDtypeStruct((n_far + blocks_here, tok_rows * heads), jnp.float32),
            jax.ShapeDtypeStruct((blocks_here + 1, n_far), jnp.int32),
        ),
        compiler_params=pltpu.CompilerParams(vmem_limit_bytes=VMEM_BYTES),
        name="table",
    )(place, chosen)


def join_call(pieces):
    in_vmem = pl.BlockSpec(memory_space=pltpu.VMEM)
    return pl.pallas_call(
        join_kernel,
        in_specs=[in_vmem] * len(pieces),
        out_specs=in_vmem,
        out_shape=jax.ShapeDtypeStruct((len(pieces),) + pieces[0].shape[1:], pieces[0].dtype),
        compiler_params=pltpu.CompilerParams(vmem_limit_bytes=VMEM_BYTES),
        name="join",
    )(*pieces)


def early_call(want, query_rows, grad_rows, own, mine, other, n_cross, n_far, heads):
    rows, width = query_rows.shape
    value_width = grad_rows.shape[1]
    tok_rows = own.shape[1]
    blocks_here = tok_rows // BLOCK
    keys = (mine.shape[0] - 1) * BLOCK + tok_rows
    tile_rows, steps = tiling(rows, n_far * BLOCK + tok_rows, heads)
    key_shape = (blocks_here, keys, width)
    by_row = [rows_of(tile_rows, width), rows_of(tile_rows, value_width)]
    return whole_call(
        functools.partial(early_kernel, n_cross, blocks_here, heads, tile_rows, steps),
        by_row + [whole(own.shape), whole(mine.shape), whole(other.shape)],
        [whole(key_shape), lanes_of(keys, tile_rows), lanes_of(keys, tile_rows), by_row[1]],
        (
            jax.ShapeDtypeStruct(key_shape, jnp.bfloat16),
            jax.ShapeDtypeStruct((keys, rows), jnp.float32),
            jax.ShapeDtypeStruct((keys, rows), jnp.float32),
            jax.ShapeDtypeStruct((rows, value_width), jnp.bfloat16),
        ),
        [pltpu.VMEM((mine.shape[0] - 1, tok_rows, width), jnp.bfloat16)],
        rows * keys * (width + value_width),
        rows * (width + value_width) * 4,
        "early_scores",
        steps,
        steps > 1,
    )(want, query_rows, grad_rows, own, mine, other)


def score_call(want, query_rows, grad_rows, bias, early, mine, other, n_far, heads, tok_rows):
    rows, width = query_rows.shape
    value_width = grad_rows.shape[1]
    blocks_here = tok_rows // BLOCK
    n_cross = mine.shape[0]
    keys = n_far * BLOCK + tok_rows
    tile_rows, steps = tiling(rows, keys, heads)
    now = jax.ShapeDtypeStruct((n_cross, width // 2, tok_rows), jnp.bfloat16)
    late = jax.ShapeDtypeStruct((1, width // 2, tok_rows), jnp.bfloat16)
    early_keys = early[0].shape[1]
    key_shape = (blocks_here, keys, width)
    return whole_call(
        functools.partial(score_kernel, n_far, n_cross, blocks_here, heads, tile_rows, steps),
        [
            rows_of(tile_rows, width),
            rows_of(tile_rows, value_width),
            lanes_of(bias.shape[0], tile_rows),
            whole(early[0].shape),
            lanes_of(early_keys, tile_rows),
            lanes_of(early_keys, tile_rows),
            whole(mine.shape),
            whole(other.shape),
        ],
        [lanes_of(keys, tile_rows), lanes_of(keys, tile_rows), whole(key_shape)]
        + [whole(s.shape) for s in (now, now, late, late)],
        (
            jax.ShapeDtypeStruct((keys, rows), jnp.bfloat16),
            jax.ShapeDtypeStruct((keys, rows), jnp.bfloat16),
            jax.ShapeDtypeStruct(key_shape, jnp.bfloat16),
            now,
            now,
            late,
            late,
        ),
        [
            pltpu.VMEM((blocks_here, (n_cross + 1) * BLOCK, width), jnp.float32),
            pltpu.VMEM((n_cross + 1, tok_rows, width), jnp.float32),
            pltpu.VMEM((n_cross, tok_rows, width), jnp.bfloat16),
        ],
        rows * keys * 2 * (width + value_width),
        rows * (width + value_width) * 4,
        "scores",
        steps,
        steps > 1,
    )(want, query_rows, grad_rows, bias, *early, mine, other)


def grad_call(want, query_rows, grad_rows, weights, grads, n_far, n_now, heads, tok_rows):
    rows, width = query_rows.shape
    value_width = grad_rows.shape[1]
    blocks_here = tok_rows // BLOCK
    n_rest = n_far - n_now
    half = jax.ShapeDtypeStruct((n_rest + 1, width // 2, tok_rows), jnp.bfloat16)
    return whole_call(
        functools.partial(grad_kernel, n_far, n_now, blocks_here, heads),
        [None] * 4,
        [None] * 2,
        (half, half),
        [
            pltpu.VMEM((blocks_here, n_rest * BLOCK + tok_rows, width), jnp.float32),
            pltpu.VMEM((n_rest + 1, tok_rows, width), jnp.float32),
        ],
        rows * (n_rest * BLOCK + tok_rows) * (width + value_width),
        rows * (width + value_width) * 4,
        "own_grads",
        1,
        rows * weights.shape[0] > UNROLLED,
    )(want, query_rows, grad_rows, weights, grads)


def out_call(keys, weights, grads, n_far, heads, value_width):
    blocks_here, count, width = keys.shape
    rows = weights.shape[1]
    tile_rows = min(OUT_ROWS if rows * count <= UNROLLED else WIDE_ROWS, BLOCK * heads)
    return call(
        functools.partial(out_kernel, n_far, blocks_here, heads),
        rows // tile_rows,
        [whole(keys.shape), lanes_of(count, tile_rows), lanes_of(count, tile_rows)],
        (rows_of(tile_rows, value_width), rows_of(tile_rows, width)),
        (
            jax.ShapeDtypeStruct((rows, value_width), jnp.bfloat16),
            jax.ShapeDtypeStruct((rows, width), jnp.bfloat16),
        ),
        [],
        rows * count * (width + value_width),
        rows * (width + value_width) * 4,
        "outputs",
    )(keys, weights, grads)


def body(queries, latent, cotangent, selection):
    tok_rows, heads, width = queries.shape
    value_width = cotangent.shape[2]
    shards = lax.axis_size("ctx")
    groups = lax.axis_size("head")
    my_shard = lax.axis_index("ctx")
    my_half = lax.axis_index("head") % 2
    blocks_here = tok_rows // BLOCK
    half = width // 2
    lines = shards // 2
    partner = [(i, i ^ 1) for i in range(groups)]
    across = [(i, i ^ 1) for i in range(shards)]

    def swap(rows):
        return lax.ppermute(rows, "head", partner)

    def up(rows, hops):
        return lax.ppermute(rows, "ctx", [(i, i + 2 * hops) for i in range(shards - 2 * hops)])

    def down(rows, hops):
        return lax.ppermute(rows, "ctx", [(i + 2 * hops, i) for i in range(shards - 2 * hops)])

    offsets = list(range(1, lines))
    cross_target = (my_shard ^ 1) - 2 * jnp.array([0] + offsets, jnp.int32)
    direct_target = my_shard - 2 * jnp.array(offsets, jnp.int32)
    n_cross, n_far = lines, shards - 1
    place = jnp.concatenate(
        [jnp.stack([my_shard, my_half]).astype(jnp.int32), cross_target, direct_target]
    )
    grad_rows = cotangent.reshape(tok_rows * heads, value_width)

    turned = latent.T
    held = lax.dynamic_slice_in_dim(turned, my_half * half, half, 0)[None]
    pieces = [held] + [up(held, k) for k in offsets]
    bias, want = table_call(place, selection.T, n_far, heads)
    *pieces, bias, want, queries = lax.optimization_barrier((*pieces, bias, want, queries))
    mine = join_call(pieces)
    mine, queries = lax.optimization_barrier((mine, queries))
    cross = lax.ppermute(mine, "ctx", across)
    query_rows = queries.reshape(tok_rows * heads, width)
    *early, grad_rows = early_call(
        want, query_rows, grad_rows, turned, mine, swap(mine), n_cross, n_far, heads
    )
    cross, early[1] = lax.optimization_barrier((cross, early[1]))
    weights, grads, keys, keep, send, late_keep, late_send = score_call(
        want, query_rows, grad_rows, bias, early, cross, swap(cross), n_far, heads, tok_rows
    )

    moving = (keep.astype(jnp.float32) + swap(send).astype(jnp.float32)).astype(jnp.bfloat16)
    moving, weights, late_send = lax.optimization_barrier((moving, weights, late_send))
    arrived = lax.ppermute(moving, "ctx", across).astype(jnp.float32)
    late_send, weights = lax.optimization_barrier((swap(late_send), weights))
    rest_keep, rest_send = grad_call(
        want, query_rows, grad_rows, weights, grads, n_far, n_cross + 1, heads, tok_rows
    )
    rest_send, weights = lax.optimization_barrier((rest_send, weights))
    late = late_keep.astype(jnp.float32) + late_send.astype(jnp.float32)
    rest = rest_keep.astype(jnp.float32) + swap(rest_send).astype(jnp.float32)
    attended, grad_queries = out_call(keys, weights, grads, n_far, heads, value_width)
    direct = [late[0]] + [rest[i] for i in range(n_far - n_cross - 1)]
    leaving = [(mine + arrived[i + 1]).astype(jnp.bfloat16) for i, mine in enumerate(direct)]
    total = rest[n_far - n_cross - 1] + arrived[0]
    *leaving, total, grad_queries = lax.optimization_barrier((*leaving, total, grad_queries))
    grad_queries = grad_queries.reshape(tok_rows, heads, width).transpose(1, 2, 0)
    for part in [down(rows, k) for k, rows in sorted(zip(offsets, leaving), key=lambda item: -item[0])]:
        total = total + part.astype(jnp.float32)
    low = total.astype(jnp.bfloat16)
    low, grad_queries = lax.optimization_barrier((low, grad_queries))
    summed = low.astype(jnp.float32)
    for j in range(1, groups // 2):
        moved = lax.ppermute(low, "head", [(i, (i + 2 * j) % groups) for i in range(groups)])
        summed = summed + moved.astype(jnp.float32)
    rest = swap(summed)
    grad_latent = jnp.where(
        my_half == 0,
        jnp.concatenate([summed, rest], axis=0),
        jnp.concatenate([rest, summed], axis=0),
    )
    return (
        attended.reshape(tok_rows, heads, value_width),
        grad_queries.transpose(2, 0, 1),
        grad_latent.T,
    )


def solution(mesh):
    placed = (P("ctx", "head", None), P("ctx", None), P("ctx", "head", None), P("ctx", None))
    return jax.shard_map(
        body,
        mesh=mesh,
        in_specs=placed,
        out_specs=(P("ctx", "head", None), P("ctx", "head", None), P("ctx", None)),
        check_vma=False,
    )
```
